32 devices in a mesh: rep: 8 (over y, x, core), mdl: 4 (over z).
Axes of the slice: x: 2, y: 2, z: 4, core: 2. Of those that a mesh axis runs over, the one named last changes fastest.
Arguments:
- token_ids: int32 [8, 512], P('rep'), may hold values from 0 to 383
- lengths: int32 [8], P('rep'), may hold values from 64 to 512
- embedding: bfloat16 [384, 2560], P(None, 'mdl'), may hold values from -105 to 105
- norm_gain: bfloat16 [2560], P('mdl'), may hold values from 0.099609375 to 1.8984375
- scores: bfloat16 [8, 32, 512, 512], P('rep', 'mdl'), may hold values from -12 to 300
- cotangent: bfloat16 [8, 512, 2560], P('rep', None, 'mdl'), may hold values from -4 to 4
- w_value: bfloat16 [2560, 2048], P(None, 'mdl'), may hold values from -0.125 to 0.125
- w_out: bfloat16 [2048, 2560], P('mdl'), may hold values from -0.125 to 0.125
- err_value: bfloat16 [8, 2560, 2048], P('rep', None, 'mdl'), may hold values from -6 to 6
- err_out: bfloat16 [8, 2048, 2560], P('rep', 'mdl'), may hold values from -6 to 6
- q_value: float32 [2048, 64], P('mdl'), may hold values from -6 to 6
- q_out: float32 [2048, 64], P('mdl'), may hold values from -6 to 6
Outputs:
- update_value: bfloat16 [2560, 2048], P(None, 'mdl')
- update_out: bfloat16 [2048, 2560], P('mdl')
- new_err_value: bfloat16 [8, 2560, 2048], P('rep', None, 'mdl')
- new_err_out: bfloat16 [8, 2048, 2560], P('rep', 'mdl')
- new_q_value: float32 [2048, 64], P('mdl')
- new_q_out: float32 [2048, 64], P('mdl')
The draws below stay inside these ranges and needn't reach their ends.
All inputs are finite; a program needn't handle non-finite values.
Results may differ from the reference program's by a relative error of at most 0.02.
Values may be sent and summed in bfloat16 or wider, within the bound.
A program may use at most 128 MiB of HBM per device.

```python
import math
import jax
import jax.numpy as jnp
import numpy as np
from jax import lax

D = 2560
HEADS = 32
HEAD_DIM = 64
VOCAB = 384
RANK = 64
SEQ = 512
SEQS = 1
INNER = 2048
SAMPLES = 8
REPLICAS = 8
N_REP = 8


def draw_embedding(key, part):
    key = jax.random.fold_in(key, 11)
    first, second = jax.random.split(key)
    columns = 10.0 ** (jnp.arange(D, dtype=jnp.float32) / D)
    row_scale = jnp.exp(jax.random.uniform(second, (VOCAB, 1), jnp.float32, 0.0, math.log(3.0)))
    base = jax.random.truncated_normal(first, -3.5, 3.5, (VOCAB, D), jnp.float32)
    return (base * row_scale * columns[None, :]).astype(jnp.bfloat16)


def draw_scores(key, part):
    key = jax.random.fold_in(key, 23)
    first = jax.random.fold_in(key, 0)
    shape = (SAMPLES, HEADS, SEQ, SEQ)
    return (2.0 * jax.random.truncated_normal(first, -6.0, 6.0, shape, jnp.float32)).astype(jnp.bfloat16)


def touch_ends(drawn, key, least, high):
    spot = [jax.random.randint(jax.random.fold_in(key, axis), (), 0, length) for axis, length in enumerate(drawn.shape)]
    widest = drawn.shape.index(max(drawn.shape))
    next_to = spot[:widest] + [(spot[widest] + 1) % drawn.shape[widest]] + spot[widest + 1:]
    return drawn.at[tuple(spot)].set(least).at[tuple(next_to)].set(high)


def block_levels(rng, extent, shards, low, largest):
    level = 1.0
    for axis_at, shards_of in shards:
        heights = jax.random.uniform(jax.random.fold_in(jax.random.fold_in(rng, 6), axis_at), (shards_of,), jnp.float32, low / len(shards), largest / len(shards))
        level = level * jnp.repeat(jnp.exp(heights), extent[axis_at] // shards_of).reshape((-1,) + (1,) * (len(extent) - 1 - axis_at))
    return level


def rank_bounds(number_of, lean):
    loads = [(1 << 20) // math.isqrt(grade ** lean) + 1 for grade in range(1, number_of + 1)]
    scale = 1 + sum(loads) // (1 << 30)
    return np.cumsum(np.array([max(1, weight // scale) for weight in loads]))


def ranked_ids(rng, dims, amount, skew):
    listing = rank_bounds(amount, skew)
    pick = jax.random.randint(jax.random.fold_in(rng, 1), dims, 0, int(listing[amount - 1]))
    rank = jnp.searchsorted(jnp.asarray(listing, jnp.int32), pick, side="right")
    return jax.random.permutation(jax.random.fold_in(rng, 2), amount)[rank].astype(jnp.int32)


def noise(key, dims, deviation, limit, cuts=(), kind=jnp.bfloat16):
    gain = block_levels(key, dims, cuts, -0.22, 0.18) if cuts else 1.0
    drawn = jax.random.normal(key, dims, jnp.float32) * deviation * gain
    return jnp.minimum(jnp.maximum(drawn, -limit), limit).astype(kind)


def setup_inputs(seed: int = 0) -> dict:
    streams_of = jax.random.split(jax.random.key(seed), 13)
    token_ids = touch_ends(ranked_ids(streams_of[0], (SAMPLES, SEQ), VOCAB, 2), jax.random.fold_in(streams_of[0], 3), 0, VOCAB - 1).astype(jnp.int32)
    lengths = touch_ends(jax.random.randint(streams_of[1], (SAMPLES,), SEQ // 8, SEQ + 1), jax.random.fold_in(streams_of[1], 1), SEQ // 8, SEQ).astype(jnp.int32)
    embedding = draw_embedding(jax.random.fold_in(streams_of[12], 71), 0)
    norm_gain = jnp.clip(1.0 + 0.18 * jax.random.normal(streams_of[3], (D,), jnp.float32), 0.099609375, 1.8984375).astype(jnp.bfloat16)
    scores = draw_scores(jax.random.fold_in(streams_of[12], 71), 0)
    cotangent = noise(streams_of[5], (SAMPLES, SEQ, D), 0.25, 4.0, ((0, 8), (2, 4)))
    w_value = noise(streams_of[6], (D, INNER), D ** -0.5, 0.125, ((1, 4),))
    w_out = noise(streams_of[7], (INNER, D), D ** -0.5, 0.125, ((0, 4),))
    err_value = noise(streams_of[8], (REPLICAS, D, INNER), 1.0, 6.0, ((0, 8), (2, 4)))
    err_out = noise(streams_of[9], (REPLICAS, INNER, D), 0.5, 6.0, ((0, 8), (1, 4)))
    q_value = noise(streams_of[10], (INNER, RANK), 1.0, 6.0, ((0, 4),), jnp.float32)
    q_out = noise(streams_of[11], (INNER, RANK), 1.0, 6.0, ((0, 4),), jnp.float32)
    return {"token_ids": token_ids, "lengths": lengths, "embedding": embedding, "norm_gain": norm_gain, "scores": scores, "cotangent": cotangent, "w_value": w_value, "w_out": w_out, "err_value": err_value, "err_out": err_out, "q_value": q_value, "q_out": q_out}


HIGH = lax.Precision.HIGHEST

def orthonormal(p):
    gram = jnp.dot(p.T, p, precision=HIGH)
    lower = jnp.linalg.cholesky(gram)
    return jax.scipy.linalg.solve_triangular(lower, p.T, lower=True).T

def reference(token_ids, lengths, embedding, norm_gain, scores, cotangent, w_value, w_out, err_value, err_out, q_value, q_out):
    x_rows = embedding[token_ids].astype(jnp.float32)
    mean_sq = lax.optimization_barrier(jnp.mean(x_rows * x_rows, axis=-1, keepdims=True))
    normed = (x_rows * lax.rsqrt(mean_sq + 1e-06) * norm_gain.astype(jnp.float32)).astype(jnp.bfloat16)
    live = jnp.arange(SEQ, dtype=jnp.int32)[None, :] < lengths[:, None]
    masked_dy = jnp.where(live[..., None], cotangent, jnp.zeros_like(cotangent))
    rows = SEQS * SEQ

    def replica(items):
        nrm, logits_in, dyr, live_r, err_v, err_o = items
        nrm2 = nrm.reshape(rows, D)
        dy2 = dyr.reshape(rows, D)
        values = jnp.dot(nrm2.astype(jnp.float32), w_value.astype(jnp.float32), preferred_element_type=jnp.float32).astype(jnp.bfloat16)
        logits = jnp.where(live_r[:, None, None, :], logits_in.astype(jnp.float32), jnp.float32(-1e+30))
        top = lax.optimization_barrier(jnp.max(logits, axis=-1, keepdims=True))
        expo = jnp.exp(logits - top)
        weights = (expo / lax.optimization_barrier(jnp.sum(expo, axis=-1, keepdims=True))).astype(jnp.bfloat16)
        values4 = values.reshape(SEQS, SEQ, HEADS, HEAD_DIM).astype(jnp.float32)
        context = jnp.einsum('shqk,skhd->sqhd', weights.astype(jnp.float32), values4).astype(jnp.bfloat16).reshape(rows, INNER)
        grad_out = jnp.dot(context.T.astype(jnp.float32), dy2.astype(jnp.float32), preferred_element_type=jnp.float32)
        dcontext = jnp.dot(dy2.astype(jnp.float32), w_out.T.astype(jnp.float32), preferred_element_type=jnp.float32).astype(jnp.bfloat16)
        dctx4 = dcontext.reshape(SEQS, SEQ, HEADS, HEAD_DIM).astype(jnp.float32)
        dvalues = jnp.einsum('shqk,sqhd->skhd', weights.astype(jnp.float32), dctx4).astype(jnp.bfloat16).reshape(rows, INNER)
        grad_value = jnp.dot(nrm2.T.astype(jnp.float32), dvalues.astype(jnp.float32), preferred_element_type=jnp.float32)
        return (grad_value + err_v.astype(jnp.float32), grad_out + err_o.astype(jnp.float32))
    mem_value, mem_out = lax.map(replica, (normed.reshape(N_REP, SEQS, SEQ, D), scores.reshape(N_REP, SEQS, HEADS, SEQ, SEQ), masked_dy.reshape(N_REP, SEQS, SEQ, D), live.reshape(N_REP, SEQS, SEQ), err_value, err_out))
    p_value = jnp.einsum('rdi,ik->dk', mem_value, q_value, precision=HIGH)
    p_out = jnp.einsum('rid,ik->dk', mem_out, q_out, precision=HIGH)
    phat_value = orthonormal(p_value)
    phat_out = orthonormal(p_out)
    new_q_value = jnp.einsum('rdi,dk->ik', mem_value, phat_value, precision=HIGH) / N_REP
    new_q_out = jnp.einsum('rid,dk->ik', mem_out, phat_out, precision=HIGH) / N_REP
    full_value = jnp.dot(phat_value, new_q_value.T, precision=HIGH)
    full_out = jnp.dot(new_q_out, phat_out.T, precision=HIGH)
    new_err_value = (mem_value - full_value[None]).astype(jnp.bfloat16)
    new_err_out = (mem_out - full_out[None]).astype(jnp.bfloat16)
    return (full_value.astype(jnp.bfloat16), full_out.astype(jnp.bfloat16), new_err_value, new_err_out, new_q_value, new_q_out)
```

```python
import functools

import jax
import jax.numpy as jnp
from jax import lax
from jax.experimental import pallas as pl
from jax.experimental.pallas import tpu as pltpu
from jax.sharding import PartitionSpec as P

HIGH = lax.Precision.HIGH
HIGHEST = lax.Precision.HIGHEST
MESH = pl.DeviceIdType.MESH
VMEM_LIMIT = 48 * 1024 * 1024


def position(chips, depth):
    me = lax.axis_index("rep")
    core = lax.rem(me, 2)
    chip = me // 2
    z = lax.axis_index("mdl")
    return me, core, chip, z


def remote(src, dst, send, recv, rep, z):
    return pltpu.make_async_remote_copy(
        src_ref=src,
        dst_ref=dst,
        send_sem=send,
        recv_sem=recv,
        device_id=(rep, z),
        device_id_type=MESH,
    )


def greet(chips, depth):
    me, core, chip, z = position(chips, depth)
    barrier = pltpu.get_barrier_semaphore()
    peers = [(chip * 2 + 1 - core, z)]
    for k in range(1, chips):
        peers.append((lax.rem(chip + k, chips) * 2 + core, z))
    for j in range(1, depth):
        peers.append((me, lax.rem(z + j, depth)))
    for peer in peers:
        pl.semaphore_signal(barrier, inc=1, device_id=peer, device_id_type=MESH)
    pl.semaphore_wait(barrier, len(peers))


def table_kernel(chips, depth, rows_ref, gain_ref, out_ref, gout_ref, sz, rz, sg, rg, sp, rp, sc, rc, local):
    me, core, chip, z = position(chips, depth)
    sibling = chip * 2 + 1 - core
    own = pltpu.make_async_copy(rows_ref, out_ref.at[z], local.at[0])
    own.start()
    own_gain = pltpu.make_async_copy(gain_ref, gout_ref.at[z], local.at[1])
    own_gain.start()
    greet(chips, depth)
    sends = []
    along = {}
    for j in range(1, depth):
        to = lax.rem(z + j, depth)
        copy = remote(rows_ref.at[me], out_ref.at[z, me], sz.at[j], rz.at[j], me, to)
        copy.start()
        gain = remote(gain_ref, gout_ref.at[z], sg.at[j], rg.at[j], me, to)
        gain.start()
        along[j] = (copy, gain)
        sends += [copy, gain]
    waits = []
    plane = {}
    for j in range(1, depth):
        along[j][0].wait_recv()
        src = lax.rem(z - j + depth, depth)
        piece = out_ref.at[src, me]
        for k in range(1, chips):
            to = lax.rem(chip + k, chips) * 2 + core
            copy = remote(piece, piece, sp.at[k, j], rp.at[k, j], to, z)
            copy.start()
            plane[k, j] = copy
            sends.append(copy)
        copy = remote(piece, piece, sc.at[0, j], rc.at[0, j], sibling, z)
        copy.start()
        waits.append(copy)
        sends.append(copy)
    for j in range(1, depth):
        src = lax.rem(z - j + depth, depth)
        for k in range(1, chips):
            plane[k, j].wait_recv()
            owner = lax.rem(chip - k + chips, chips) * 2 + core
            piece = out_ref.at[src, owner]
            copy = remote(piece, piece, sc.at[k, j], rc.at[k, j], sibling, z)
            copy.start()
            waits.append(copy)
            sends.append(copy)
    own.wait()
    own_gain.wait()
    for j in range(1, depth):
        along[j][1].wait_recv()
    for copy in waits:
        copy.wait_recv()
    for copy in sends:
        copy.wait_send()


def gather_table(embedding, norm_gain, replicas, depth):
    chips = replicas // 2
    vocab, width = embedding.shape
    rows = embedding.reshape(replicas, vocab // replicas, width)
    gain = jnp.broadcast_to(norm_gain[None, :], (16, width))
    whole = jax.ShapeDtypeStruct((depth,) + rows.shape, rows.dtype)
    gains = jax.ShapeDtypeStruct((depth, 16, width), gain.dtype)
    sem = pltpu.SemaphoreType.DMA
    table, gains = pl.pallas_call(
        functools.partial(table_kernel, chips, depth),
        out_shape=(whole, gains),
        in_specs=[pl.BlockSpec(memory_space=pltpu.VMEM)] * 2,
        out_specs=[pl.BlockSpec(memory_space=pltpu.VMEM)] * 2,
        scratch_shapes=[
            sem((depth,)),
            sem((depth,)),
            sem((depth,)),
            sem((depth,)),
            sem((chips, depth)),
            sem((chips, depth)),
            sem((chips, depth)),
            sem((chips, depth)),
            sem((2,)),
        ],
        compiler_params=pltpu.CompilerParams(
            collective_id=0, has_side_effects=True, vmem_limit_bytes=VMEM_LIMIT
        ),
    )(rows, gain)
    table = table.reshape(depth, vocab, width).transpose(1, 0, 2).reshape(vocab, depth * width)
    return table, gains[:, 0, :].reshape(depth * width)


def reduce_steps(chips, depth, p_ref, out_ref, b1, b2, b3, sems, between):
    s1, r1, s2, r2, s3, r3, s4, r4, s5, r5, s6, r6 = sems
    me, core, chip, z = position(chips, depth)
    sibling = chip * 2 + 1 - core
    greet(chips, depth)
    sends = []
    first = remote(p_ref.at[1 - core], b1, s1.at[0], r1.at[0], sibling, z)
    first.start()
    sends.append(first)
    between(0)
    first.wait_recv()
    b1[...] = b1[...] + p_ref[core]
    group = []
    for k in range(1, chips):
        to = lax.rem(chip + k, chips)
        copy = remote(b1.at[to], b2.at[chip], s2.at[k], r2.at[k], to * 2 + core, z)
        copy.start()
        group.append(copy)
    sends += group
    between(1)
    total = b1[chip]
    for k in range(1, chips):
        group[k - 1].wait_recv()
        total = total + b2[lax.rem(chip - k + chips, chips)]
    if depth > 1:
        b2[chip] = total
        group = []
        for j in range(1, depth):
            to = lax.rem(z + j, depth)
            copy = remote(b2.at[chip, to], b3.at[z], s3.at[j], r3.at[j], me, to)
            copy.start()
            group.append(copy)
        sends += group
        total = b2[chip, z]
        for j in range(1, depth):
            group[j - 1].wait_recv()
            total = total + b3[lax.rem(z - j + depth, depth)]
        out_ref[core, chip, z] = total
    else:
        out_ref[core, chip] = total
    zz = z if depth > 1 else 0
    along = {}
    for j in range(1, depth):
        piece = out_ref.at[core, chip, zz]
        copy = remote(piece, piece, s4.at[j], r4.at[j], me, lax.rem(z + j, depth))
        copy.start()
        along[j] = copy
        sends.append(copy)
    waits = []
    plane = {}
    for j in range(depth):
        if j:
            along[j].wait_recv()
        src = lax.rem(zz - j + depth, depth) if depth > 1 else 0
        piece = out_ref.at[core, chip, src]
        for k in range(1, chips):
            to = lax.rem(chip + k, chips) * 2 + core
            copy = remote(piece, piece, s5.at[k, j], r5.at[k, j], to, z)
            copy.start()
            plane[k, j] = copy
            sends.append(copy)
        copy = remote(piece, piece, s6.at[0, j], r6.at[0, j], sibling, z)
        copy.start()
        waits.append(copy)
        sends.append(copy)
    between(2)
    for j in range(depth):
        src = lax.rem(zz - j + depth, depth) if depth > 1 else 0
        for k in range(1, chips):
            plane[k, j].wait_recv()
            piece = out_ref.at[core, lax.rem(chip - k + chips, chips), src]
            copy = remote(piece, piece, s6.at[k, j], r6.at[k, j], sibling, z)
            copy.start()
            waits.append(copy)
            sends.append(copy)
    between(3)
    for copy in waits:
        copy.wait_recv()
    for copy in sends:
        copy.wait_send()


def reduce_scratch(chips, depth, rows):
    sem = pltpu.SemaphoreType.DMA
    return [
        pltpu.VMEM((chips, depth, rows, 128), jnp.float32),
        pltpu.VMEM((chips, depth, rows, 128), jnp.float32),
        pltpu.VMEM((depth, rows, 128), jnp.float32),
        sem((1,)),
        sem((1,)),
        sem((chips,)),
        sem((chips,)),
        sem((depth,)),
        sem((depth,)),
        sem((depth,)),
        sem((depth,)),
        sem((chips, depth)),
        sem((chips, depth)),
        sem((chips, depth)),
        sem((chips, depth)),
    ]


def left_kernel(chips, depth, p_ref, out_ref, b1, b2, b3, *sems):
    reduce_steps(chips, depth, p_ref, out_ref, b1, b2, b3, sems, lambda stage: None)


def reduce_left(p, replicas, depth):
    chips = replicas // 2
    rows = p.shape[0] // (2 * chips * depth)
    shape = (2, chips, depth, rows, 128)
    out = pl.pallas_call(
        functools.partial(left_kernel, chips, depth),
        out_shape=jax.ShapeDtypeStruct(shape, jnp.float32),
        in_specs=[pl.BlockSpec(memory_space=pltpu.VMEM)],
        out_specs=pl.BlockSpec(memory_space=pltpu.VMEM),
        scratch_shapes=reduce_scratch(chips, depth, rows),
        compiler_params=pltpu.CompilerParams(
            collective_id=1, has_side_effects=True, vmem_limit_bytes=VMEM_LIMIT
        ),
    )(p.reshape(shape))
    return out.reshape(p.shape)


def factor_steps(work, rank, begin, end):
    tiles = [[work[h * rank + 8 * t : h * rank + 8 * t + 8, :] for t in range(rank // 8)] for h in range(2)]
    lines = lax.broadcasted_iota(jnp.int32, (8, 128), 0)
    for j in range(begin, end):
        at, line = divmod(j, 8)
        for h in range(2):
            lane = j + (rank if h == 0 else 0)
            part = tiles[h]
            pivot = part[at][line : line + 1, lane : lane + 1]
            inverse = 1.0 / jnp.sqrt(pivot)
            row = part[at][line : line + 1, :] * inverse
            for t in range(at, rank // 8):
                tile = part[t]
                column = tile[:, lane : lane + 1] * inverse
                fresh = tile - column * row
                if t == at:
                    fresh = jnp.where(lines > line, fresh, jnp.where(lines == line, row, tile))
                part[t] = fresh
    for h in range(2):
        for t in range(rank // 8):
            work[h * rank + 8 * t : h * rank + 8 * t + 8, :] = tiles[h][t]


def right_kernel(chips, rank, p_ref, gram_ref, out_ref, low_ref, b1, b2, b3, work, *sems):
    def between(stage):
        if stage == 0:
            work[...] = gram_ref[...]
        factor_steps(work, rank, stage * rank // 4, (stage + 1) * rank // 4)

    reduce_steps(chips, 1, p_ref, out_ref, b1, b2, b3, sems, between)
    lanes = lax.broadcasted_iota(jnp.int32, (rank, 128), 1)
    low_ref[:rank, :] = jnp.where(lanes < rank, work[:rank, :], 0.0)
    low_ref[rank:, :] = jnp.where(lanes >= rank, work[rank:, :], 0.0)


def reduce_right(p, gram, replicas):
    chips = replicas // 2
    rank = gram.shape[0] // 2
    rows = p.shape[0] // (2 * chips)
    shape = (2, chips, 1, rows, 128)
    eye = jnp.eye(rank, dtype=jnp.float32)
    start = jnp.concatenate(
        [
            jnp.concatenate([eye, gram[:rank, :rank]], axis=1),
            jnp.concatenate([gram[rank:, rank:], eye], axis=1),
        ],
        axis=0,
    )
    out, low = pl.pallas_call(
        functools.partial(right_kernel, chips, rank),
        out_shape=(
            jax.ShapeDtypeStruct(shape, jnp.float32),
            jax.ShapeDtypeStruct((2 * rank, 128), jnp.float32),
        ),
        in_specs=[pl.BlockSpec(memory_space=pltpu.VMEM)] * 2,
        out_specs=[pl.BlockSpec(memory_space=pltpu.VMEM)] * 2,
        scratch_shapes=(lambda s: s[:3] + [pltpu.VMEM((2 * rank, 128), jnp.float32)] + s[3:])(
            reduce_scratch(chips, 1, rows)
        ),
        compiler_params=pltpu.CompilerParams(
            collective_id=2, has_side_effects=True, vmem_limit_bytes=VMEM_LIMIT
        ),
    )(p.reshape(shape), start)
    return out.reshape(p.shape), low


def shards(
    replicas,
    depth,
    token_ids,
    lengths,
    embedding,
    norm_gain,
    scores,
    cotangent,
    w_value,
    w_out,
    err_value,
    err_out,
    q_value,
    q_out,
):
    samples, seq = token_ids.shape
    vocab = embedding.shape[0]
    rows = samples * seq
    rank = q_value.shape[1]
    dy_whole = lax.all_gather(cotangent, "mdl", axis=2, tiled=True)
    width_full = dy_whole.shape[2]
    raw, gain = gather_table(embedding, norm_gain, replicas, depth)
    raw = raw.astype(jnp.float32)
    scale = lax.rsqrt(jnp.sum(raw * raw, axis=1) / width_full + 1e-06)
    table = (raw * scale[:, None] * gain.astype(jnp.float32)[None, :]).astype(jnp.bfloat16)
    flat_ids = token_ids.reshape(rows)
    onehot = (flat_ids[:, None] == jnp.arange(vocab, dtype=jnp.int32)[None, :]).astype(jnp.bfloat16)
    normed = jnp.dot(onehot, table, preferred_element_type=jnp.float32).astype(jnp.bfloat16)
    live = jnp.arange(seq, dtype=jnp.int32)[None, :] < lengths[:, None]
    heads_local = scores.shape[1]
    inner_local = w_value.shape[1]
    head_size = inner_local // heads_local
    values = jnp.dot(normed, w_value, preferred_element_type=jnp.float32).astype(jnp.bfloat16)
    logits = jnp.where(live[:, None, None, :], scores.astype(jnp.float32), jnp.float32(-1e30))
    top = jnp.max(logits, axis=-1, keepdims=True)
    expo = jnp.exp(logits - top)
    weights = (expo / jnp.sum(expo, axis=-1, keepdims=True)).astype(jnp.bfloat16)
    values4 = values.reshape(samples, seq, heads_local, head_size)
    context = (
        jnp.einsum("shqk,skhd->sqhd", weights, values4, preferred_element_type=jnp.float32)
        .astype(jnp.bfloat16)
        .reshape(rows, inner_local)
    )
    dy_rows = jnp.where(live[..., None], dy_whole, jnp.zeros_like(dy_whole)).reshape(
        rows, width_full
    )
    dcontext = lax.dot_general(
        dy_rows, w_out, (((1,), (1,)), ((), ())), preferred_element_type=jnp.float32
    ).astype(jnp.bfloat16)
    dctx4 = dcontext.reshape(samples, seq, heads_local, head_size)
    dvalues = (
        jnp.einsum("shqk,sqhd->skhd", weights, dctx4, preferred_element_type=jnp.float32)
        .astype(jnp.bfloat16)
        .reshape(rows, inner_local)
    )
    grad_out = lax.dot_general(
        context, dy_rows, (((0,), (0,)), ((), ())), preferred_element_type=jnp.float32
    )
    grad_value = lax.dot_general(
        normed, dvalues, (((0,), (0,)), ((), ())), preferred_element_type=jnp.float32
    )
    mem_value = grad_value + err_value[0].astype(jnp.float32)
    mem_out = grad_out + err_out[0].astype(jnp.float32)
    p_value = jnp.dot(mem_value, q_value, precision=HIGH)
    p_out = lax.dot_general(mem_out, q_out, (((0,), (0,)), ((), ())), precision=HIGH)
    p_both = reduce_left(jnp.concatenate([p_value, p_out], axis=1), replicas, depth)
    gram = lax.dot_general(p_both, p_both, (((0,), (0,)), ((), ())), precision=HIGHEST)
    term_value = lax.dot_general(
        mem_value, p_both[:, :rank], (((0,), (0,)), ((), ())), precision=HIGH
    )
    term_out = jnp.dot(mem_out, p_both[:, rank:], precision=HIGH)
    terms, low = reduce_right(jnp.concatenate([term_value, term_out], axis=1), gram, replicas)
    phat = lax.dot_general(p_both, low, (((1,), (1,)), ((), ())), precision=HIGHEST)
    new_q = lax.dot_general(terms, low, (((1,), (1,)), ((), ())), precision=HIGHEST) / replicas
    new_q_value = new_q[:, :rank]
    new_q_out = new_q[:, rank:]
    full_value = lax.dot_general(
        phat[:, :rank], new_q_value, (((1,), (1,)), ((), ())), precision=HIGH
    )
    full_out = lax.dot_general(
        new_q_out, phat[:, rank:], (((1,), (1,)), ((), ())), precision=HIGH
    )
    new_err_value = (mem_value - full_value).astype(jnp.bfloat16)[None]
    new_err_out = (mem_out - full_out).astype(jnp.bfloat16)[None]
    return (
        full_value.astype(jnp.bfloat16),
        full_out.astype(jnp.bfloat16),
        new_err_value,
        new_err_out,
        new_q_value,
        new_q_out,
    )


def solution(mesh):
    return jax.shard_map(
        functools.partial(shards, mesh.shape["rep"], mesh.shape["mdl"]),
        mesh=mesh,
        in_specs=(
            P("rep", None),
            P("rep"),
            P(None, "mdl"),
            P("mdl"),
            P("rep", "mdl", None, None),
            P("rep", None, "mdl"),
            P(None, "mdl"),
            P("mdl", None),
            P("rep", None, "mdl"),
            P("rep", "mdl", None),
            P("mdl", None),
            P("mdl", None),
        ),
        out_specs=(
            P(None, "mdl"),
            P("mdl", None),
            P("rep", None, "mdl"),
            P("rep", "mdl", None),
            P("mdl", None),
            P("mdl", None),
        ),
        check_vma=False,
    )
```

```python
import functools

import jax
import jax.numpy as jnp
from jax import lax
from jax.experimental import pallas as pl
from jax.experimental.pallas import tpu as pltpu
from jax.sharding import PartitionSpec as P

HIGH = lax.Precision.HIGH
HIGHEST = lax.Precision.HIGHEST
MESH = pl.DeviceIdType.MESH
VMEM_LIMIT = 48 * 1024 * 1024


def position(chips, depth):
    me = lax.axis_index("rep")
    core = lax.rem(me, 2)
    chip = me // 2
    z = lax.axis_index("mdl")
    return me, core, chip, z


def remote(src, dst, send, recv, rep, z):
    return pltpu.make_async_remote_copy(
        src_ref=src,
        dst_ref=dst,
        send_sem=send,
        recv_sem=recv,
        device_id=(rep, z),
        device_id_type=MESH,
    )


def greet(chips, depth):
    me, core, chip, z = position(chips, depth)
    barrier = pltpu.get_barrier_semaphore()
    peers = [(chip * 2 + 1 - core, z)]
    for k in range(1, chips):
        peers.append((lax.rem(chip + k, chips) * 2 + core, z))
    for j in range(1, depth):
        peers.append((me, lax.rem(z + j, depth)))
    for peer in peers:
        pl.semaphore_signal(barrier, inc=1, device_id=peer, device_id_type=MESH)
    pl.semaphore_wait(barrier, len(peers))


def table_kernel(chips, depth, rows_ref, gain_ref, out_ref, gout_ref, sz, rz, sg, rg, sp, rp, sc, rc, local):
    me, core, chip, z = position(chips, depth)
    sibling = chip * 2 + 1 - core
    width = rows_ref.shape[2]

    def spot(owner, src):
        return out_ref.at[owner, :, pl.ds(pl.multiple_of(src * width, 128), width)]

    own = pltpu.make_async_copy(
        rows_ref, out_ref.at[:, :, pl.ds(pl.multiple_of(z * width, 128), width)], local.at[0]
    )
    own.start()
    own_gain = pltpu.make_async_copy(gain_ref, gout_ref.at[z], local.at[1])
    own_gain.start()
    greet(chips, depth)
    sends = []
    along = {}
    for j in range(1, depth):
        to = lax.rem(z + j, depth)
        copy = remote(rows_ref.at[me], spot(me, z), sz.at[j], rz.at[j], me, to)
        copy.start()
        gain = remote(gain_ref, gout_ref.at[z], sg.at[j], rg.at[j], me, to)
        gain.start()
        along[j] = (copy, gain)
        sends += [copy, gain]
    waits = []
    plane = {}
    for j in range(1, depth):
        along[j][0].wait_recv()
        src = lax.rem(z - j + depth, depth)
        piece = spot(me, src)
        for k in range(1, chips):
            to = lax.rem(chip + k, chips) * 2 + core
            copy = remote(piece, piece, sp.at[k, j], rp.at[k, j], to, z)
            copy.start()
            plane[k, j] = copy
            sends.append(copy)
        copy = remote(piece, piece, sc.at[0, j], rc.at[0, j], sibling, z)
        copy.start()
        waits.append(copy)
        sends.append(copy)
    for j in range(1, depth):
        src = lax.rem(z - j + depth, depth)
        for k in range(1, chips):
            plane[k, j].wait_recv()
            owner = lax.rem(chip - k + chips, chips) * 2 + core
            piece = spot(owner, src)
            copy = remote(piece, piece, sc.at[k, j], rc.at[k, j], sibling, z)
            copy.start()
            waits.append(copy)
            sends.append(copy)
    own.wait()
    own_gain.wait()
    for j in range(1, depth):
        along[j][1].wait_recv()
    for copy in waits:
        copy.wait_recv()
    for copy in sends:
        copy.wait_send()


def gather_table(embedding, norm_gain, replicas, depth):
    chips = replicas // 2
    vocab, width = embedding.shape
    rows = embedding.reshape(replicas, vocab // replicas, width)
    gain = jnp.broadcast_to(norm_gain[None, :], (16, width))
    whole = jax.ShapeDtypeStruct(rows.shape[:2] + (depth * width,), rows.dtype)
    gains = jax.ShapeDtypeStruct((depth, 16, width), gain.dtype)
    sem = pltpu.SemaphoreType.DMA
    table, gains = pl.pallas_call(
        functools.partial(table_kernel, chips, depth),
        out_shape=(whole, gains),
        in_specs=[pl.BlockSpec(memory_space=pltpu.VMEM)] * 2,
        out_specs=[pl.BlockSpec(memory_space=pltpu.VMEM)] * 2,
        scratch_shapes=[
            sem((depth,)),
            sem((depth,)),
            sem((depth,)),
            sem((depth,)),
            sem((chips, depth)),
            sem((chips, depth)),
            sem((chips, depth)),
            sem((chips, depth)),
            sem((2,)),
        ],
        compiler_params=pltpu.CompilerParams(
            collective_id=0, has_side_effects=True, vmem_limit_bytes=VMEM_LIMIT
        ),
    )(rows, gain)
    table = table.reshape(vocab, depth * width)
    return table, gains[:, 0, :].reshape(depth * width)


def reduce_steps(chips, depth, p_ref, out_ref, b1, b2, b3, sems, between):
    s1, r1, s2, r2, s3, r3, s4, r4, s5, r5, s6, r6 = sems
    me, core, chip, z = position(chips, depth)
    sibling = chip * 2 + 1 - core
    greet(chips, depth)
    sends = []
    first = remote(p_ref.at[1 - core], b1, s1.at[0], r1.at[0], sibling, z)
    first.start()
    sends.append(first)
    between(0)
    first.wait_recv()
    kind = p_ref.dtype
    b1[...] = (b1[...].astype(jnp.float32) + p_ref[core].astype(jnp.float32)).astype(kind)
    group = []
    for k in range(1, chips):
        to = lax.rem(chip + k, chips)
        copy = remote(b1.at[to], b2.at[chip], s2.at[k], r2.at[k], to * 2 + core, z)
        copy.start()
        group.append(copy)
    sends += group
    between(1)
    total = b1[chip].astype(jnp.float32)
    for k in range(1, chips):
        group[k - 1].wait_recv()
        total = total + b2[lax.rem(chip - k + chips, chips)].astype(jnp.float32)
    if depth > 1:
        b2[chip] = total.astype(kind)
        group = []
        for j in range(1, depth):
            to = lax.rem(z + j, depth)
            copy = remote(b2.at[chip, to], b3.at[z], s3.at[j], r3.at[j], me, to)
            copy.start()
            group.append(copy)
        sends += group
        total = b2[chip, z].astype(jnp.float32)
        for j in range(1, depth):
            group[j - 1].wait_recv()
            total = total + b3[lax.rem(z - j + depth, depth)].astype(jnp.float32)
        out_ref[core, chip, z] = total.astype(kind)
    else:
        out_ref[core, chip] = total.astype(kind)
    zz = z if depth > 1 else 0
    along = {}
    for j in range(1, depth):
        piece = out_ref.at[core, chip, zz]
        copy = remote(piece, piece, s4.at[j], r4.at[j], me, lax.rem(z + j, depth))
        copy.start()
        along[j] = copy
        sends.append(copy)
    waits = []
    plane = {}
    for j in range(depth):
        if j:
            along[j].wait_recv()
        src = lax.rem(zz - j + depth, depth) if depth > 1 else 0
        piece = out_ref.at[core, chip, src]
        for k in range(1, chips):
            to = lax.rem(chip + k, chips) * 2 + core
            copy = remote(piece, piece, s5.at[k, j], r5.at[k, j], to, z)
            copy.start()
            plane[k, j] = copy
            sends.append(copy)
        copy = remote(piece, piece, s6.at[0, j], r6.at[0, j], sibling, z)
        copy.start()
        waits.append(copy)
        sends.append(copy)
    between(2)
    for j in range(depth):
        src = lax.rem(zz - j + depth, depth) if depth > 1 else 0
        for k in range(1, chips):
            plane[k, j].wait_recv()
            piece = out_ref.at[core, lax.rem(chip - k + chips, chips), src]
            copy = remote(piece, piece, s6.at[k, j], r6.at[k, j], sibling, z)
            copy.start()
            waits.append(copy)
            sends.append(copy)
    between(3)
    for copy in waits:
        copy.wait_recv()
    for copy in sends:
        copy.wait_send()


def reduce_scratch(chips, depth, rows, kind):
    sem = pltpu.SemaphoreType.DMA
    return [
        pltpu.VMEM((chips, depth, rows, 128), kind),
        pltpu.VMEM((chips, depth, rows, 128), kind),
        pltpu.VMEM((depth, rows, 128), kind),
        sem((1,)),
        sem((1,)),
        sem((chips,)),
        sem((chips,)),
        sem((depth,)),
        sem((depth,)),
        sem((depth,)),
        sem((depth,)),
        sem((chips, depth)),
        sem((chips, depth)),
        sem((chips, depth)),
        sem((chips, depth)),
    ]


def left_kernel(chips, depth, p_ref, out_ref, b1, b2, b3, *sems):
    reduce_steps(chips, depth, p_ref, out_ref, b1, b2, b3, sems, lambda stage: None)


def reduce_left(p, replicas, depth):
    chips = replicas // 2
    rows = p.shape[0] // (2 * chips * depth)
    shape = (2, chips, depth, rows, 128)
    out = pl.pallas_call(
        functools.partial(left_kernel, chips, depth),
        out_shape=jax.ShapeDtypeStruct(shape, p.dtype),
        in_specs=[pl.BlockSpec(memory_space=pltpu.VMEM)],
        out_specs=pl.BlockSpec(memory_space=pltpu.VMEM),
        scratch_shapes=reduce_scratch(chips, depth, rows, p.dtype),
        compiler_params=pltpu.CompilerParams(
            collective_id=1, has_side_effects=True, vmem_limit_bytes=VMEM_LIMIT
        ),
    )(p.reshape(shape))
    return out.reshape(p.shape)


def factor_steps(work, rank, begin, end):
    tiles = [[work[h * rank + 8 * t : h * rank + 8 * t + 8, :] for t in range(rank // 8)] for h in range(2)]
    lines = lax.broadcasted_iota(jnp.int32, (8, 128), 0)
    for j in range(begin, end):
        at, line = divmod(j, 8)
        for h in range(2):
            lane = j + (rank if h == 0 else 0)
            part = tiles[h]
            pivot = part[at][line : line + 1, lane : lane + 1]
            inverse = 1.0 / jnp.sqrt(pivot)
            row = part[at][line : line + 1, :] * inverse
            for t in range(at, rank // 8):
                tile = part[t]
                column = tile[:, lane : lane + 1] * inverse
                fresh = tile - column * row
                if t == at:
                    fresh = jnp.where(lines > line, fresh, jnp.where(lines == line, row, tile))
                part[t] = fresh
    for h in range(2):
        for t in range(rank // 8):
            work[h * rank + 8 * t : h * rank + 8 * t + 8, :] = tiles[h][t]


def right_kernel(chips, rank, p_ref, gram_ref, out_ref, low_ref, b1, b2, b3, work, *sems):
    def between(stage):
        if stage == 0:
            work[...] = gram_ref[...]
        factor_steps(work, rank, stage * rank // 4, (stage + 1) * rank // 4)

    reduce_steps(chips, 1, p_ref, out_ref, b1, b2, b3, sems, between)
    lanes = lax.broadcasted_iota(jnp.int32, (rank, 128), 1)
    low_ref[:rank, :] = jnp.where(lanes < rank, work[:rank, :], 0.0)
    low_ref[rank:, :] = jnp.where(lanes >= rank, work[rank:, :], 0.0)


def reduce_right(p, gram, replicas):
    chips = replicas // 2
    rank = gram.shape[0] // 2
    rows = p.shape[0] // (2 * chips)
    shape = (2, chips, 1, rows, 128)
    eye = jnp.eye(rank, dtype=jnp.float32)
    start = jnp.concatenate(
        [
            jnp.concatenate([eye, gram[:rank, :rank]], axis=1),
            jnp.concatenate([gram[rank:, rank:], eye], axis=1),
        ],
        axis=0,
    )
    out, low = pl.pallas_call(
        functools.partial(right_kernel, chips, rank),
        out_shape=(
            jax.ShapeDtypeStruct(shape, jnp.float32),
            jax.ShapeDtypeStruct((2 * rank, 128), jnp.float32),
        ),
        in_specs=[pl.BlockSpec(memory_space=pltpu.VMEM)] * 2,
        out_specs=[pl.BlockSpec(memory_space=pltpu.VMEM)] * 2,
        scratch_shapes=(lambda s: s[:3] + [pltpu.VMEM((2 * rank, 128), jnp.float32)] + s[3:])(
            reduce_scratch(chips, 1, rows, p.dtype)
        ),
        compiler_params=pltpu.CompilerParams(
            collective_id=2, has_side_effects=True, vmem_limit_bytes=VMEM_LIMIT
        ),
    )(p.reshape(shape), start)
    return out.reshape(p.shape), low


def shards(
    replicas,
    depth,
    token_ids,
    lengths,
    embedding,
    norm_gain,
    scores,
    cotangent,
    w_value,
    w_out,
    err_value,
    err_out,
    q_value,
    q_out,
):
    samples, seq = token_ids.shape
    vocab = embedding.shape[0]
    rows = samples * seq
    rank = q_value.shape[1]
    spot = lax.axis_index("mdl")
    live = jnp.arange(seq, dtype=jnp.int32)[None, :] < lengths[:, None]
    masked = jnp.where(live[..., None], cotangent, jnp.zeros_like(cotangent)).reshape(rows, -1)
    width = masked.shape[1]
    width_full = width * depth
    pieces = [masked]
    for j in range(1, depth):
        pieces.append(lax.ppermute(masked, "mdl", [(i, (i + j) % depth) for i in range(depth)]))
    raw, gain = gather_table(embedding, norm_gain, replicas, depth)
    raw = raw.astype(jnp.float32)
    scale = lax.rsqrt(jnp.sum(raw * raw, axis=1) / width_full + 1e-06)
    table = (raw * scale[:, None] * gain.astype(jnp.float32)[None, :]).astype(jnp.bfloat16)
    flat_ids = token_ids.reshape(rows)
    onehot = (flat_ids[:, None] == jnp.arange(vocab, dtype=jnp.int32)[None, :]).astype(jnp.bfloat16)
    normed = jnp.dot(onehot, table, preferred_element_type=jnp.float32).astype(jnp.bfloat16)
    heads_local = scores.shape[1]
    inner_local = w_value.shape[1]
    head_size = inner_local // heads_local
    values = jnp.dot(normed, w_value, preferred_element_type=jnp.float32).astype(jnp.bfloat16)
    logits = jnp.where(live[:, None, None, :], scores.astype(jnp.float32), jnp.float32(-1e30))
    top = jnp.max(logits, axis=-1, keepdims=True)
    expo = jnp.exp(logits - top)
    weights = (expo / jnp.sum(expo, axis=-1, keepdims=True)).astype(jnp.bfloat16)
    values4 = values.reshape(samples, seq, heads_local, head_size)
    context = (
        jnp.einsum("shqk,skhd->sqhd", weights, values4, preferred_element_type=jnp.float32)
        .astype(jnp.bfloat16)
        .reshape(rows, inner_local)
    )
    dy_rows = jnp.zeros((rows, width_full), jnp.bfloat16)
    for j in (0, 1, 3, 2) if depth == 4 else range(depth):
        source = lax.rem(spot - j + depth, depth)
        dy_rows = lax.dynamic_update_slice(dy_rows, pieces[j], (0, source * width))
    dcontext = lax.dot_general(
        dy_rows, w_out, (((1,), (1,)), ((), ())), preferred_element_type=jnp.float32
    ).astype(jnp.bfloat16)
    dctx4 = dcontext.reshape(samples, seq, heads_local, head_size)
    dvalues = (
        jnp.einsum("shqk,sqhd->skhd", weights, dctx4, preferred_element_type=jnp.float32)
        .astype(jnp.bfloat16)
        .reshape(rows, inner_local)
    )
    grad_out = lax.dot_general(
        context, dy_rows, (((0,), (0,)), ((), ())), preferred_element_type=jnp.float32
    )
    grad_value = lax.dot_general(
        normed, dvalues, (((0,), (0,)), ((), ())), preferred_element_type=jnp.float32
    )
    mem_value = grad_value + err_value[0].astype(jnp.float32)
    mem_out = grad_out + err_out[0].astype(jnp.float32)
    kept_value = mem_value.astype(jnp.bfloat16)
    kept_out = mem_out.astype(jnp.bfloat16)
    none = jnp.zeros_like(q_value)
    right_value = jnp.concatenate([q_value, none], axis=1).astype(jnp.bfloat16)
    right_out = jnp.concatenate([none, q_out], axis=1).astype(jnp.bfloat16)
    part = jnp.dot(kept_value, right_value, preferred_element_type=jnp.float32)
    part = part + lax.dot_general(
        kept_out, right_out, (((0,), (0,)), ((), ())), preferred_element_type=jnp.float32
    )
    p_both = reduce_left(part.astype(jnp.bfloat16), replicas, depth)
    gram = lax.dot_general(
        p_both, p_both, (((0,), (0,)), ((), ())), preferred_element_type=jnp.float32
    )
    first = jnp.arange(2 * rank)[None, :] < rank
    nothing = jnp.zeros_like(p_both)
    term = lax.dot_general(
        kept_value,
        jnp.where(first, p_both, nothing),
        (((0,), (0,)), ((), ())),
        preferred_element_type=jnp.float32,
    )
    term = term + jnp.dot(
        kept_out, jnp.where(first, nothing, p_both), preferred_element_type=jnp.float32
    )
    terms, low = reduce_right(term, gram, replicas)
    phat = lax.dot_general(
        p_both.astype(jnp.float32), low, (((1,), (1,)), ((), ())), precision=HIGH
    )
    new_q = lax.dot_general(terms, low, (((1,), (1,)), ((), ())), precision=HIGHEST) / replicas
    new_q_value = new_q[:, :rank]
    new_q_out = new_q[:, rank:]
    rough_phat = phat.astype(jnp.bfloat16)
    rough_q = new_q.astype(jnp.bfloat16)
    full_value = lax.dot_general(
        rough_phat[:, :rank],
        rough_q[:, :rank],
        (((1,), (1,)), ((), ())),
        preferred_element_type=jnp.float32,
    )
    full_out = lax.dot_general(
        rough_q[:, rank:],
        rough_phat[:, rank:],
        (((1,), (1,)), ((), ())),
        preferred_element_type=jnp.float32,
    )
    new_err_value = (mem_value - full_value).astype(jnp.bfloat16)[None]
    new_err_out = (mem_out - full_out).astype(jnp.bfloat16)[None]
    return (
        full_value.astype(jnp.bfloat16),
        full_out.astype(jnp.bfloat16),
        new_err_value,
        new_err_out,
        new_q_value,
        new_q_out,
    )


def solution(mesh):
    return jax.shard_map(
        functools.partial(shards, mesh.shape["rep"], mesh.shape["mdl"]),
        mesh=mesh,
        in_specs=(
            P("rep", None),
            P("rep"),
            P(None, "mdl"),
            P("mdl"),
            P("rep", "mdl", None, None),
            P("rep", None, "mdl"),
            P(None, "mdl"),
            P("mdl", None),
            P("rep", None, "mdl"),
            P("rep", "mdl", None),
            P("mdl", None),
            P("mdl", None),
        ),
        out_specs=(
            P(None, "mdl"),
            P("mdl", None),
            P("rep", None, "mdl"),
            P("rep", "mdl", None),
            P("mdl", None),
            P("mdl", None),
        ),
        check_vma=False,
    )
```

```python
import functools

import jax
import jax.numpy as jnp
from jax import lax
from jax.experimental import pallas as pl
from jax.experimental.pallas import tpu as pltpu
from jax.sharding import PartitionSpec as P

HIGH = lax.Precision.HIGH
HIGHEST = lax.Precision.HIGHEST
MESH = pl.DeviceIdType.MESH
VMEM_LIMIT = 48 * 1024 * 1024


def position(chips, depth):
    me = lax.axis_index("rep")
    core = lax.rem(me, 2)
    chip = me // 2
    z = lax.axis_index("mdl")
    return me, core, chip, z


def remote(src, dst, send, recv, rep, z):
    return pltpu.make_async_remote_copy(
        src_ref=src,
        dst_ref=dst,
        send_sem=send,
        recv_sem=recv,
        device_id=(rep, z),
        device_id_type=MESH,
    )


def greet(chips, depth):
    me, core, chip, z = position(chips, depth)
    barrier = pltpu.get_barrier_semaphore()
    peers = [(chip * 2 + 1 - core, z)]
    for k in range(1, chips):
        peers.append((lax.rem(chip + k, chips) * 2 + core, z))
    for j in range(1, depth):
        peers.append((me, lax.rem(z + j, depth)))
    for peer in peers:
        pl.semaphore_signal(barrier, inc=1, device_id=peer, device_id_type=MESH)
    pl.semaphore_wait(barrier, len(peers))


def table_kernel(chips, depth, rows_ref, gain_ref, out_ref, gout_ref, sz, rz, sg, rg, sp, rp, sc, rc, local):
    me, core, chip, z = position(chips, depth)
    sibling = chip * 2 + 1 - core
    width = rows_ref.shape[2]

    def spot(owner, src):
        return out_ref.at[owner, :, pl.ds(pl.multiple_of(src * width, 128), width)]

    own = pltpu.make_async_copy(
        rows_ref, out_ref.at[:, :, pl.ds(pl.multiple_of(z * width, 128), width)], local.at[0]
    )
    own.start()
    own_gain = pltpu.make_async_copy(gain_ref, gout_ref.at[z], local.at[1])
    own_gain.start()
    greet(chips, depth)
    sends = []
    along = {}
    for j in range(1, depth):
        to = lax.rem(z + j, depth)
        copy = remote(rows_ref.at[me], spot(me, z), sz.at[j], rz.at[j], me, to)
        copy.start()
        gain = remote(gain_ref, gout_ref.at[z], sg.at[j], rg.at[j], me, to)
        gain.start()
        along[j] = (copy, gain)
        sends += [copy, gain]
    waits = []
    plane = {}
    for j in range(1, depth):
        along[j][0].wait_recv()
        src = lax.rem(z - j + depth, depth)
        piece = spot(me, src)
        for k in range(1, chips):
            to = lax.rem(chip + k, chips) * 2 + core
            copy = remote(piece, piece, sp.at[k, j], rp.at[k, j], to, z)
            copy.start()
            plane[k, j] = copy
            sends.append(copy)
        copy = remote(piece, piece, sc.at[0, j], rc.at[0, j], sibling, z)
        copy.start()
        waits.append(copy)
        sends.append(copy)
    for j in range(1, depth):
        src = lax.rem(z - j + depth, depth)
        for k in range(1, chips):
            plane[k, j].wait_recv()
            owner = lax.rem(chip - k + chips, chips) * 2 + core
            piece = spot(owner, src)
            copy = remote(piece, piece, sc.at[k, j], rc.at[k, j], sibling, z)
            copy.start()
            waits.append(copy)
            sends.append(copy)
    own.wait()
    own_gain.wait()
    for j in range(1, depth):
        along[j][1].wait_recv()
    for copy in waits:
        copy.wait_recv()
    for copy in sends:
        copy.wait_send()


def gather_table(embedding, norm_gain, replicas, depth):
    chips = replicas // 2
    vocab, width = embedding.shape
    rows = embedding.reshape(replicas, vocab // replicas, width)
    gain = jnp.broadcast_to(norm_gain[None, :], (16, width))
    whole = jax.ShapeDtypeStruct(rows.shape[:2] + (depth * width,), rows.dtype)
    gains = jax.ShapeDtypeStruct((depth, 16, width), gain.dtype)
    sem = pltpu.SemaphoreType.DMA
    table, gains = pl.pallas_call(
        functools.partial(table_kernel, chips, depth),
        out_shape=(whole, gains),
        in_specs=[pl.BlockSpec(memory_space=pltpu.VMEM)] * 2,
        out_specs=[pl.BlockSpec(memory_space=pltpu.VMEM)] * 2,
        scratch_shapes=[
            sem((depth,)),
            sem((depth,)),
            sem((depth,)),
            sem((depth,)),
            sem((chips, depth)),
            sem((chips, depth)),
            sem((chips, depth)),
            sem((chips, depth)),
            sem((2,)),
        ],
        compiler_params=pltpu.CompilerParams(
            collective_id=0, has_side_effects=True, vmem_limit_bytes=VMEM_LIMIT
        ),
    )(rows, gain)
    table = table.reshape(vocab, depth * width)
    return table, gains[:, 0, :].reshape(depth * width)


def reduce_steps(chips, depth, p_ref, out_ref, b1, b2, b3, sems, between):
    s1, r1, s2, r2, s3, r3, s4, r4, s5, r5, s6, r6 = sems
    me, core, chip, z = position(chips, depth)
    sibling = chip * 2 + 1 - core
    greet(chips, depth)
    sends = []
    first = remote(p_ref.at[1 - core], b1, s1.at[0], r1.at[0], sibling, z)
    first.start()
    sends.append(first)
    between(0)
    first.wait_recv()
    kind = p_ref.dtype
    b1[...] = (b1[...].astype(jnp.float32) + p_ref[core].astype(jnp.float32)).astype(kind)
    group = []
    for k in range(1, chips):
        to = lax.rem(chip + k, chips)
        copy = remote(b1.at[to], b2.at[chip], s2.at[k], r2.at[k], to * 2 + core, z)
        copy.start()
        group.append(copy)
    sends += group
    between(1)
    total = b1[chip].astype(jnp.float32)
    for k in range(1, chips):
        group[k - 1].wait_recv()
        total = total + b2[lax.rem(chip - k + chips, chips)].astype(jnp.float32)
    if depth > 1:
        b2[chip] = total.astype(kind)
        group = []
        for j in range(1, depth):
            to = lax.rem(z + j, depth)
            copy = remote(b2.at[chip, to], b3.at[z], s3.at[j], r3.at[j], me, to)
            copy.start()
            group.append(copy)
        sends += group
        total = b2[chip, z].astype(jnp.float32)
        for j in range(1, depth):
            group[j - 1].wait_recv()
            total = total + b3[lax.rem(z - j + depth, depth)].astype(jnp.float32)
        out_ref[core, chip, z] = total.astype(kind)
    else:
        out_ref[core, chip] = total.astype(kind)
    zz = z if depth > 1 else 0
    along = {}
    for j in range(1, depth):
        piece = out_ref.at[core, chip, zz]
        copy = remote(piece, piece, s4.at[j], r4.at[j], me, lax.rem(z + j, depth))
        copy.start()
        along[j] = copy
        sends.append(copy)
    waits = []
    plane = {}
    for j in range(depth):
        if j:
            along[j].wait_recv()
        src = lax.rem(zz - j + depth, depth) if depth > 1 else 0
        piece = out_ref.at[core, chip, src]
        for k in range(1, chips):
            to = lax.rem(chip + k, chips) * 2 + core
            copy = remote(piece, piece, s5.at[k, j], r5.at[k, j], to, z)
            copy.start()
            plane[k, j] = copy
            sends.append(copy)
        copy = remote(piece, piece, s6.at[0, j], r6.at[0, j], sibling, z)
        copy.start()
        waits.append(copy)
        sends.append(copy)
    between(2)
    for j in range(depth):
        src = lax.rem(zz - j + depth, depth) if depth > 1 else 0
        for k in range(1, chips):
            plane[k, j].wait_recv()
            piece = out_ref.at[core, lax.rem(chip - k + chips, chips), src]
            copy = remote(piece, piece, s6.at[k, j], r6.at[k, j], sibling, z)
            copy.start()
            waits.append(copy)
            sends.append(copy)
    between(3)
    for copy in waits:
        copy.wait_recv()
    for copy in sends:
        copy.wait_send()


def reduce_scratch(chips, depth, rows, kind):
    sem = pltpu.SemaphoreType.DMA
    return [
        pltpu.VMEM((chips, depth, rows, 128), kind),
        pltpu.VMEM((chips, depth, rows, 128), kind),
        pltpu.VMEM((depth, rows, 128), kind),
        sem((1,)),
        sem((1,)),
        sem((chips,)),
        sem((chips,)),
        sem((depth,)),
        sem((depth,)),
        sem((depth,)),
        sem((depth,)),
        sem((chips, depth)),
        sem((chips, depth)),
        sem((chips, depth)),
        sem((chips, depth)),
    ]


def left_kernel(chips, depth, p_ref, out_ref, b1, b2, b3, *sems):
    reduce_steps(chips, depth, p_ref, out_ref, b1, b2, b3, sems, lambda stage: None)


def reduce_left(p, replicas, depth):
    chips = replicas // 2
    rows = p.shape[0] // (2 * chips * depth)
    shape = (2, chips, depth, rows, 128)
    out = pl.pallas_call(
        functools.partial(left_kernel, chips, depth),
        out_shape=jax.ShapeDtypeStruct(shape, p.dtype),
        in_specs=[pl.BlockSpec(memory_space=pltpu.VMEM)],
        out_specs=pl.BlockSpec(memory_space=pltpu.VMEM),
        scratch_shapes=reduce_scratch(chips, depth, rows, p.dtype),
        compiler_params=pltpu.CompilerParams(
            collective_id=1, has_side_effects=True, vmem_limit_bytes=VMEM_LIMIT
        ),
    )(p.reshape(shape))
    return out.reshape(p.shape)


def factor_steps(work, rank, begin, end):
    tiles = [[work[h * rank + 8 * t : h * rank + 8 * t + 8, :] for t in range(rank // 8)] for h in range(2)]
    lines = lax.broadcasted_iota(jnp.int32, (8, 128), 0)
    for j in range(begin, end):
        at, line = divmod(j, 8)
        for h in range(2):
            lane = j + (rank if h == 0 else 0)
            part = tiles[h]
            pivot = part[at][line : line + 1, lane : lane + 1]
            inverse = 1.0 / jnp.sqrt(pivot)
            row = part[at][line : line + 1, :] * inverse
            for t in range(at, rank // 8):
                tile = part[t]
                column = tile[:, lane : lane + 1] * inverse
                fresh = tile - column * row
                if t == at:
                    fresh = jnp.where(lines > line, fresh, jnp.where(lines == line, row, tile))
                part[t] = fresh
    for h in range(2):
        for t in range(rank // 8):
            work[h * rank + 8 * t : h * rank + 8 * t + 8, :] = tiles[h][t]


def right_kernel(chips, rank, p_ref, gram_ref, out_ref, low_ref, b1, b2, b3, work, *sems):
    def between(stage):
        if stage == 0:
            work[...] = gram_ref[...]
        factor_steps(work, rank, stage * rank // 4, (stage + 1) * rank // 4)

    reduce_steps(chips, 1, p_ref, out_ref, b1, b2, b3, sems, between)
    lanes = lax.broadcasted_iota(jnp.int32, (rank, 128), 1)
    low_ref[:rank, :] = jnp.where(lanes < rank, work[:rank, :], 0.0)
    low_ref[rank:, :] = jnp.where(lanes >= rank, work[rank:, :], 0.0)


def reduce_right(p, gram, replicas):
    chips = replicas // 2
    rank = gram.shape[0] // 2
    rows = p.shape[0] // (2 * chips)
    shape = (2, chips, 1, rows, 128)
    eye = jnp.eye(rank, dtype=jnp.float32)
    start = jnp.concatenate(
        [
            jnp.concatenate([eye, gram[:rank, :rank]], axis=1),
            jnp.concatenate([gram[rank:, rank:], eye], axis=1),
        ],
        axis=0,
    )
    out, low = pl.pallas_call(
        functools.partial(right_kernel, chips, rank),
        out_shape=(
            jax.ShapeDtypeStruct(shape, jnp.float32),
            jax.ShapeDtypeStruct((2 * rank, 128), jnp.float32),
        ),
        in_specs=[pl.BlockSpec(memory_space=pltpu.VMEM)] * 2,
        out_specs=[pl.BlockSpec(memory_space=pltpu.VMEM)] * 2,
        scratch_shapes=(lambda s: s[:3] + [pltpu.VMEM((2 * rank, 128), jnp.float32)] + s[3:])(
            reduce_scratch(chips, 1, rows, p.dtype)
        ),
        compiler_params=pltpu.CompilerParams(
            collective_id=2, has_side_effects=True, vmem_limit_bytes=VMEM_LIMIT
        ),
    )(p.reshape(shape), start)
    return out.reshape(p.shape), low


def shards(
    replicas,
    depth,
    token_ids,
    lengths,
    embedding,
    norm_gain,
    scores,
    cotangent,
    w_value,
    w_out,
    err_value,
    err_out,
    q_value,
    q_out,
):
    samples, seq = token_ids.shape
    vocab = embedding.shape[0]
    rows = samples * seq
    rank = q_value.shape[1]
    dy_whole = lax.all_gather(cotangent, "mdl", axis=2, tiled=True)
    width_full = dy_whole.shape[2]
    raw, gain = gather_table(embedding, norm_gain, replicas, depth)
    raw = raw.astype(jnp.float32)
    scale = lax.rsqrt(jnp.sum(raw * raw, axis=1) / width_full + 1e-06)
    table = (raw * scale[:, None] * gain.astype(jnp.float32)[None, :]).astype(jnp.bfloat16)
    flat_ids = token_ids.reshape(rows)
    onehot = (flat_ids[:, None] == jnp.arange(vocab, dtype=jnp.int32)[None, :]).astype(jnp.bfloat16)
    normed = jnp.dot(onehot, table, preferred_element_type=jnp.float32).astype(jnp.bfloat16)
    live = jnp.arange(seq, dtype=jnp.int32)[None, :] < lengths[:, None]
    heads_local = scores.shape[1]
    inner_local = w_value.shape[1]
    head_size = inner_local // heads_local
    values = jnp.dot(normed, w_value, preferred_element_type=jnp.float32).astype(jnp.bfloat16)
    logits = jnp.where(live[:, None, None, :], scores.astype(jnp.float32), jnp.float32(-1e30))
    top = jnp.max(logits, axis=-1, keepdims=True)
    expo = jnp.exp(logits - top)
    weights = (expo / jnp.sum(expo, axis=-1, keepdims=True)).astype(jnp.bfloat16)
    values4 = values.reshape(samples, seq, heads_local, head_size)
    context = (
        jnp.einsum("shqk,skhd->sqhd", weights, values4, preferred_element_type=jnp.float32)
        .astype(jnp.bfloat16)
        .reshape(rows, inner_local)
    )
    dy_rows = jnp.where(live[..., None], dy_whole, jnp.zeros_like(dy_whole)).reshape(
        rows, width_full
    )
    dcontext = lax.dot_general(
        dy_rows, w_out, (((1,), (1,)), ((), ())), preferred_element_type=jnp.float32
    ).astype(jnp.bfloat16)
    dctx4 = dcontext.reshape(samples, seq, heads_local, head_size)
    dvalues = (
        jnp.einsum("shqk,sqhd->skhd", weights, dctx4, preferred_element_type=jnp.float32)
        .astype(jnp.bfloat16)
        .reshape(rows, inner_local)
    )
    grad_out = lax.dot_general(
        context, dy_rows, (((0,), (0,)), ((), ())), preferred_element_type=jnp.float32
    )
    grad_value = lax.dot_general(
        normed, dvalues, (((0,), (0,)), ((), ())), preferred_element_type=jnp.float32
    )
    mem_value = grad_value + err_value[0].astype(jnp.float32)
    mem_out = grad_out + err_out[0].astype(jnp.float32)
    kept_value = mem_value.astype(jnp.bfloat16)
    kept_out = mem_out.astype(jnp.bfloat16)
    none = jnp.zeros_like(q_value)
    right_value = jnp.concatenate([q_value, none], axis=1).astype(jnp.bfloat16)
    right_out = jnp.concatenate([none, q_out], axis=1).astype(jnp.bfloat16)
    part = jnp.dot(kept_value, right_value, preferred_element_type=jnp.float32)
    part = part + lax.dot_general(
        kept_out, right_out, (((0,), (0,)), ((), ())), preferred_element_type=jnp.float32
    )
    p_both = reduce_left(part.astype(jnp.bfloat16), replicas, depth)
    gram = lax.dot_general(
        p_both, p_both, (((0,), (0,)), ((), ())), preferred_element_type=jnp.float32
    )
    first = jnp.arange(2 * rank)[None, :] < rank
    nothing = jnp.zeros_like(p_both)
    term = lax.dot_general(
        kept_value,
        jnp.where(first, p_both, nothing),
        (((0,), (0,)), ((), ())),
        preferred_element_type=jnp.float32,
    )
    term = term + jnp.dot(
        kept_out, jnp.where(first, nothing, p_both), preferred_element_type=jnp.float32
    )
    terms, low = reduce_right(term, gram, replicas)
    phat = lax.dot_general(
        p_both.astype(jnp.float32), low, (((1,), (1,)), ((), ())), precision=HIGH
    )
    new_q = lax.dot_general(terms, low, (((1,), (1,)), ((), ())), precision=HIGHEST) / replicas
    new_q_value = new_q[:, :rank]
    new_q_out = new_q[:, rank:]
    rough_phat = phat.astype(jnp.bfloat16)
    rough_q = new_q.astype(jnp.bfloat16)
    full_value = lax.dot_general(
        rough_phat[:, :rank],
        rough_q[:, :rank],
        (((1,), (1,)), ((), ())),
        preferred_element_type=jnp.float32,
    )
    full_out = lax.dot_general(
        rough_q[:, rank:],
        rough_phat[:, rank:],
        (((1,), (1,)), ((), ())),
        preferred_element_type=jnp.float32,
    )
    new_err_value = (mem_value - full_value).astype(jnp.bfloat16)[None]
    new_err_out = (mem_out - full_out).astype(jnp.bfloat16)[None]
    return (
        full_value.astype(jnp.bfloat16),
        full_out.astype(jnp.bfloat16),
        new_err_value,
        new_err_out,
        new_q_value,
        new_q_out,
    )


def solution(mesh):
    return jax.shard_map(
        functools.partial(shards, mesh.shape["rep"], mesh.shape["mdl"]),
        mesh=mesh,
        in_specs=(
            P("rep", None),
            P("rep"),
            P(None, "mdl"),
            P("mdl"),
            P("rep", "mdl", None, None),
            P("rep", None, "mdl"),
            P(None, "mdl"),
            P("mdl", None),
            P("rep", None, "mdl"),
            P("rep", "mdl", None),
            P("mdl", None),
            P("mdl", None),
        ),
        out_specs=(
            P(None, "mdl"),
            P("mdl", None),
            P("rep", None, "mdl"),
            P("rep", "mdl", None),
            P("mdl", None),
            P("mdl", None),
        ),
        check_vma=False,
    )
```

```python
import functools

import jax
import jax.numpy as jnp
from jax import lax
from jax.experimental import pallas as pl
from jax.experimental.pallas import tpu as pltpu
from jax.sharding import PartitionSpec as P

HIGH = lax.Precision.HIGH
HIGHEST = lax.Precision.HIGHEST
MESH = pl.DeviceIdType.MESH
VMEM_LIMIT = 48 * 1024 * 1024


def position(chips, depth):
    me = lax.axis_index("rep")
    core = lax.rem(me, 2)
    chip = me // 2
    z = lax.axis_index("mdl")
    return me, core, chip, z


def remote(src, dst, send, recv, rep, z):
    return pltpu.make_async_remote_copy(
        src_ref=src,
        dst_ref=dst,
        send_sem=send,
        recv_sem=recv,
        device_id=(rep, z),
        device_id_type=MESH,
    )


def greet(chips, depth):
    me, core, chip, z = position(chips, depth)
    barrier = pltpu.get_barrier_semaphore()
    peers = [(chip * 2 + 1 - core, z)]
    for k in range(1, chips):
        peers.append((lax.rem(chip + k, chips) * 2 + core, z))
    for j in range(1, depth):
        peers.append((me, lax.rem(z + j, depth)))
    for peer in peers:
        pl.semaphore_signal(barrier, inc=1, device_id=peer, device_id_type=MESH)
    pl.semaphore_wait(barrier, len(peers))


def table_kernel(chips, depth, rows_ref, gain_ref, out_ref, gout_ref, sz, rz, sg, rg, sp, rp, sc, rc, local):
    me, core, chip, z = position(chips, depth)
    sibling = chip * 2 + 1 - core
    width = rows_ref.shape[2]

    def spot(owner, src):
        return out_ref.at[owner, :, pl.ds(pl.multiple_of(src * width, 128), width)]

    own = pltpu.make_async_copy(
        rows_ref, out_ref.at[:, :, pl.ds(pl.multiple_of(z * width, 128), width)], local.at[0]
    )
    own.start()
    own_gain = pltpu.make_async_copy(gain_ref, gout_ref.at[z], local.at[1])
    own_gain.start()
    greet(chips, depth)
    sends = []
    along = {}
    for j in range(1, depth):
        to = lax.rem(z + j, depth)
        copy = remote(rows_ref.at[me], spot(me, z), sz.at[j], rz.at[j], me, to)
        copy.start()
        gain = remote(gain_ref, gout_ref.at[z], sg.at[j], rg.at[j], me, to)
        gain.start()
        along[j] = (copy, gain)
        sends += [copy, gain]
    waits = []
    plane = {}
    for j in range(1, depth):
        along[j][0].wait_recv()
        src = lax.rem(z - j + depth, depth)
        piece = spot(me, src)
        for k in range(1, chips):
            to = lax.rem(chip + k, chips) * 2 + core
            copy = remote(piece, piece, sp.at[k, j], rp.at[k, j], to, z)
            copy.start()
            plane[k, j] = copy
            sends.append(copy)
        copy = remote(piece, piece, sc.at[0, j], rc.at[0, j], sibling, z)
        copy.start()
        waits.append(copy)
        sends.append(copy)
    for j in range(1, depth):
        src = lax.rem(z - j + depth, depth)
        for k in range(1, chips):
            plane[k, j].wait_recv()
            owner = lax.rem(chip - k + chips, chips) * 2 + core
            piece = spot(owner, src)
            copy = remote(piece, piece, sc.at[k, j], rc.at[k, j], sibling, z)
            copy.start()
            waits.append(copy)
            sends.append(copy)
    own.wait()
    own_gain.wait()
    for j in range(1, depth):
        along[j][1].wait_recv()
    for copy in waits:
        copy.wait_recv()
    for copy in sends:
        copy.wait_send()


def gather_table(embedding, norm_gain, replicas, depth):
    chips = replicas // 2
    vocab, width = embedding.shape
    rows = embedding.reshape(replicas, vocab // replicas, width)
    gain = jnp.broadcast_to(norm_gain[None, :], (16, width))
    whole = jax.ShapeDtypeStruct(rows.shape[:2] + (depth * width,), rows.dtype)
    gains = jax.ShapeDtypeStruct((depth, 16, width), gain.dtype)
    sem = pltpu.SemaphoreType.DMA
    table, gains = pl.pallas_call(
        functools.partial(table_kernel, chips, depth),
        out_shape=(whole, gains),
        in_specs=[pl.BlockSpec(memory_space=pltpu.VMEM)] * 2,
        out_specs=[pl.BlockSpec(memory_space=pltpu.VMEM)] * 2,
        scratch_shapes=[
            sem((depth,)),
            sem((depth,)),
            sem((depth,)),
            sem((depth,)),
            sem((chips, depth)),
            sem((chips, depth)),
            sem((chips, depth)),
            sem((chips, depth)),
            sem((2,)),
        ],
        compiler_params=pltpu.CompilerParams(
            collective_id=0, has_side_effects=True, vmem_limit_bytes=VMEM_LIMIT
        ),
    )(rows, gain)
    table = table.reshape(vocab, depth * width)
    return table, gains[:, 0, :].reshape(depth * width)


def reduce_steps(chips, depth, p_ref, out_ref, b1, b2, b3, sems, between):
    s1, r1, s2, r2, s3, r3, s4, r4, s5, r5, s6, r6 = sems
    me, core, chip, z = position(chips, depth)
    sibling = chip * 2 + 1 - core
    greet(chips, depth)
    sends = []
    first = remote(p_ref.at[1 - core], b1, s1.at[0], r1.at[0], sibling, z)
    first.start()
    sends.append(first)
    between(0)
    first.wait_recv()
    kind = p_ref.dtype
    b1[...] = (b1[...].astype(jnp.float32) + p_ref[core].astype(jnp.float32)).astype(kind)
    group = []
    for k in range(1, chips):
        to = lax.rem(chip + k, chips)
        copy = remote(b1.at[to], b2.at[chip], s2.at[k], r2.at[k], to * 2 + core, z)
        copy.start()
        group.append(copy)
    sends += group
    between(1)
    total = b1[chip].astype(jnp.float32)
    for k in range(1, chips):
        group[k - 1].wait_recv()
        total = total + b2[lax.rem(chip - k + chips, chips)].astype(jnp.float32)
    if depth > 1:
        b2[chip] = total.astype(kind)
        group = []
        for j in range(1, depth):
            to = lax.rem(z + j, depth)
            copy = remote(b2.at[chip, to], b3.at[z], s3.at[j], r3.at[j], me, to)
            copy.start()
            group.append(copy)
        sends += group
        total = b2[chip, z].astype(jnp.float32)
        for j in range(1, depth):
            group[j - 1].wait_recv()
            total = total + b3[lax.rem(z - j + depth, depth)].astype(jnp.float32)
        out_ref[core, chip, z] = total.astype(kind)
    else:
        out_ref[core, chip] = total.astype(kind)
    zz = z if depth > 1 else 0
    along = {}
    for j in range(1, depth):
        piece = out_ref.at[core, chip, zz]
        copy = remote(piece, piece, s4.at[j], r4.at[j], me, lax.rem(z + j, depth))
        copy.start()
        along[j] = copy
        sends.append(copy)
    waits = []
    plane = {}
    for j in range(depth):
        if j:
            along[j].wait_recv()
        src = lax.rem(zz - j + depth, depth) if depth > 1 else 0
        piece = out_ref.at[core, chip, src]
        for k in range(1, chips):
            to = lax.rem(chip + k, chips) * 2 + core
            copy = remote(piece, piece, s5.at[k, j], r5.at[k, j], to, z)
            copy.start()
            plane[k, j] = copy
            sends.append(copy)
        copy = remote(piece, piece, s6.at[0, j], r6.at[0, j], sibling, z)
        copy.start()
        waits.append(copy)
        sends.append(copy)
    between(2)
    for j in range(depth):
        src = lax.rem(zz - j + depth, depth) if depth > 1 else 0
        for k in range(1, chips):
            plane[k, j].wait_recv()
            piece = out_ref.at[core, lax.rem(chip - k + chips, chips), src]
            copy = remote(piece, piece, s6.at[k, j], r6.at[k, j], sibling, z)
            copy.start()
            waits.append(copy)
            sends.append(copy)
    between(3)
    for copy in waits:
        copy.wait_recv()
    for copy in sends:
        copy.wait_send()


def reduce_scratch(chips, depth, rows, kind):
    sem = pltpu.SemaphoreType.DMA
    return [
        pltpu.VMEM((chips, depth, rows, 128), kind),
        pltpu.VMEM((chips, depth, rows, 128), kind),
        pltpu.VMEM((depth, rows, 128), kind),
        sem((1,)),
        sem((1,)),
        sem((chips,)),
        sem((chips,)),
        sem((depth,)),
        sem((depth,)),
        sem((depth,)),
        sem((depth,)),
        sem((chips, depth)),
        sem((chips, depth)),
        sem((chips, depth)),
        sem((chips, depth)),
    ]


def left_kernel(chips, depth, p_ref, out_ref, b1, b2, b3, *sems):
    reduce_steps(chips, depth, p_ref, out_ref, b1, b2, b3, sems, lambda stage: None)


def reduce_left(p, replicas, depth):
    chips = replicas // 2
    rows = p.shape[0] // (2 * chips * depth)
    shape = (2, chips, depth, rows, 128)
    out = pl.pallas_call(
        functools.partial(left_kernel, chips, depth),
        out_shape=jax.ShapeDtypeStruct(shape, p.dtype),
        in_specs=[pl.BlockSpec(memory_space=pltpu.VMEM)],
        out_specs=pl.BlockSpec(memory_space=pltpu.VMEM),
        scratch_shapes=reduce_scratch(chips, depth, rows, p.dtype),
        compiler_params=pltpu.CompilerParams(
            collective_id=1, has_side_effects=True, vmem_limit_bytes=VMEM_LIMIT
        ),
    )(p.reshape(shape))
    return out.reshape(p.shape)


def factor_steps(work, rank, begin, end):
    tiles = [[work[h * rank + 8 * t : h * rank + 8 * t + 8, :] for t in range(rank // 8)] for h in range(2)]
    lines = lax.broadcasted_iota(jnp.int32, (8, 128), 0)
    for j in range(begin, end):
        at, line = divmod(j, 8)
        for h in range(2):
            lane = j + (rank if h == 0 else 0)
            part = tiles[h]
            row = part[at][line : line + 1, :]
            columns = [
                jnp.broadcast_to(part[t][:, lane : lane + 1], (8, 128))
                for t in range(at, rank // 8)
            ]
            scaled = row * (1.0 / columns[0][line : line + 1, :])
            for t in range(at, rank // 8):
                fresh = part[t] - columns[t - at] * scaled
                if t == at:
                    fresh = jnp.where(lines > line, fresh, part[t])
                part[t] = fresh
    for h in range(2):
        for t in range(rank // 8):
            work[h * rank + 8 * t : h * rank + 8 * t + 8, :] = tiles[h][t]


def right_kernel(chips, rank, p_ref, gram_ref, out_ref, low_ref, b1, b2, b3, work, *sems):
    def between(stage):
        if stage == 0:
            work[...] = gram_ref[...]
        factor_steps(work, rank, stage * rank // 4, (stage + 1) * rank // 4)

    reduce_steps(chips, 1, p_ref, out_ref, b1, b2, b3, sems, between)
    lanes = lax.broadcasted_iota(jnp.int32, (rank, 128), 1)
    lines = lax.broadcasted_iota(jnp.int32, (rank, 128), 0)
    top = work[:rank, :]
    pivots = jnp.sum(jnp.where(lanes == lines + rank, top, 0.0), axis=1, keepdims=True)
    low_ref[:rank, :] = jnp.where(lanes < rank, top / jnp.sqrt(pivots), 0.0)
    end = work[rank:, :]
    pivots = jnp.sum(jnp.where(lanes == lines, end, 0.0), axis=1, keepdims=True)
    low_ref[rank:, :] = jnp.where(lanes >= rank, end / jnp.sqrt(pivots), 0.0)


def reduce_right(p, gram, replicas):
    chips = replicas // 2
    rank = gram.shape[0] // 2
    rows = p.shape[0] // (2 * chips)
    shape = (2, chips, 1, rows, 128)
    eye = jnp.eye(rank, dtype=jnp.float32)
    start = jnp.concatenate(
        [
            jnp.concatenate([eye, gram[:rank, :rank]], axis=1),
            jnp.concatenate([gram[rank:, rank:], eye], axis=1),
        ],
        axis=0,
    )
    out, low = pl.pallas_call(
        functools.partial(right_kernel, chips, rank),
        out_shape=(
            jax.ShapeDtypeStruct(shape, jnp.float32),
            jax.ShapeDtypeStruct((2 * rank, 128), jnp.float32),
        ),
        in_specs=[pl.BlockSpec(memory_space=pltpu.VMEM)] * 2,
        out_specs=[pl.BlockSpec(memory_space=pltpu.VMEM)] * 2,
        scratch_shapes=(lambda s: s[:3] + [pltpu.VMEM((2 * rank, 128), jnp.float32)] + s[3:])(
            reduce_scratch(chips, 1, rows, p.dtype)
        ),
        compiler_params=pltpu.CompilerParams(
            collective_id=2, has_side_effects=True, vmem_limit_bytes=VMEM_LIMIT
        ),
    )(p.reshape(shape), start)
    return out.reshape(p.shape), low


def shards(
    replicas,
    depth,
    token_ids,
    lengths,
    embedding,
    norm_gain,
    scores,
    cotangent,
    w_value,
    w_out,
    err_value,
    err_out,
    q_value,
    q_out,
):
    samples, seq = token_ids.shape
    vocab = embedding.shape[0]
    rows = samples * seq
    rank = q_value.shape[1]
    dy_whole = lax.all_gather(cotangent, "mdl", axis=2, tiled=True)
    width_full = dy_whole.shape[2]
    raw, gain = gather_table(embedding, norm_gain, replicas, depth)
    raw = raw.astype(jnp.float32)
    scale = lax.rsqrt(jnp.sum(raw * raw, axis=1) / width_full + 1e-06)
    table = (raw * scale[:, None] * gain.astype(jnp.float32)[None, :]).astype(jnp.bfloat16)
    flat_ids = token_ids.reshape(rows)
    onehot = (flat_ids[:, None] == jnp.arange(vocab, dtype=jnp.int32)[None, :]).astype(jnp.bfloat16)
    normed = jnp.dot(onehot, table, preferred_element_type=jnp.float32).astype(jnp.bfloat16)
    live = jnp.arange(seq, dtype=jnp.int32)[None, :] < lengths[:, None]
    heads_local = scores.shape[1]
    inner_local = w_value.shape[1]
    head_size = inner_local // heads_local
    values = jnp.dot(normed, w_value, preferred_element_type=jnp.float32).astype(jnp.bfloat16)
    logits = jnp.where(live[:, None, None, :], scores.astype(jnp.float32), jnp.float32(-1e30))
    top = jnp.max(logits, axis=-1, keepdims=True)
    expo = jnp.exp(logits - top)
    weights = (expo / jnp.sum(expo, axis=-1, keepdims=True)).astype(jnp.bfloat16)
    values4 = values.reshape(samples, seq, heads_local, head_size)
    context = (
        jnp.einsum("shqk,skhd->sqhd", weights, values4, preferred_element_type=jnp.float32)
        .astype(jnp.bfloat16)
        .reshape(rows, inner_local)
    )
    dy_rows = jnp.where(live[..., None], dy_whole, jnp.zeros_like(dy_whole)).reshape(
        rows, width_full
    )
    dcontext = lax.dot_general(
        dy_rows, w_out, (((1,), (1,)), ((), ())), preferred_element_type=jnp.float32
    ).astype(jnp.bfloat16)
    dctx4 = dcontext.reshape(samples, seq, heads_local, head_size)
    dvalues = (
        jnp.einsum("shqk,sqhd->skhd", weights, dctx4, preferred_element_type=jnp.float32)
        .astype(jnp.bfloat16)
        .reshape(rows, inner_local)
    )
    grad_out = lax.dot_general(
        context, dy_rows, (((0,), (0,)), ((), ())), preferred_element_type=jnp.float32
    )
    grad_value = lax.dot_general(
        normed, dvalues, (((0,), (0,)), ((), ())), preferred_element_type=jnp.float32
    )
    mem_value = grad_value + err_value[0].astype(jnp.float32)
    mem_out = grad_out + err_out[0].astype(jnp.float32)
    kept_value = mem_value.astype(jnp.bfloat16)
    kept_out = mem_out.astype(jnp.bfloat16)
    none = jnp.zeros_like(q_value)
    right_value = jnp.concatenate([q_value, none], axis=1).astype(jnp.bfloat16)
    right_out = jnp.concatenate([none, q_out], axis=1).astype(jnp.bfloat16)
    part = jnp.dot(kept_value, right_value, preferred_element_type=jnp.float32)
    part = part + lax.dot_general(
        kept_out, right_out, (((0,), (0,)), ((), ())), preferred_element_type=jnp.float32
    )
    p_both = reduce_left(part.astype(jnp.bfloat16), replicas, depth)
    gram = lax.dot_general(
        p_both, p_both, (((0,), (0,)), ((), ())), preferred_element_type=jnp.float32
    )
    first = jnp.arange(2 * rank)[None, :] < rank
    nothing = jnp.zeros_like(p_both)
    term = lax.dot_general(
        kept_value,
        jnp.where(first, p_both, nothing),
        (((0,), (0,)), ((), ())),
        preferred_element_type=jnp.float32,
    )
    term = term + jnp.dot(
        kept_out, jnp.where(first, nothing, p_both), preferred_element_type=jnp.float32
    )
    terms, low = reduce_right(term, gram, replicas)
    phat = lax.dot_general(
        p_both.astype(jnp.float32), low, (((1,), (1,)), ((), ())), precision=HIGH
    )
    new_q = lax.dot_general(terms, low, (((1,), (1,)), ((), ())), precision=HIGHEST) / replicas
    new_q_value = new_q[:, :rank]
    new_q_out = new_q[:, rank:]
    rough_phat = phat.astype(jnp.bfloat16)
    rough_q = new_q.astype(jnp.bfloat16)
    full_value = lax.dot_general(
        rough_phat[:, :rank],
        rough_q[:, :rank],
        (((1,), (1,)), ((), ())),
        preferred_element_type=jnp.float32,
    )
    full_out = lax.dot_general(
        rough_q[:, rank:],
        rough_phat[:, rank:],
        (((1,), (1,)), ((), ())),
        preferred_element_type=jnp.float32,
    )
    new_err_value = (mem_value - full_value).astype(jnp.bfloat16)[None]
    new_err_out = (mem_out - full_out).astype(jnp.bfloat16)[None]
    return (
        full_value.astype(jnp.bfloat16),
        full_out.astype(jnp.bfloat16),
        new_err_value,
        new_err_out,
        new_q_value,
        new_q_out,
    )


def solution(mesh):
    return jax.shard_map(
        functools.partial(shards, mesh.shape["rep"], mesh.shape["mdl"]),
        mesh=mesh,
        in_specs=(
            P("rep", None),
            P("rep"),
            P(None, "mdl"),
            P("mdl"),
            P("rep", "mdl", None, None),
            P("rep", None, "mdl"),
            P(None, "mdl"),
            P("mdl", None),
            P("rep", None, "mdl"),
            P("rep", "mdl", None),
            P("mdl", None),
            P("mdl", None),
        ),
        out_specs=(
            P(None, "mdl"),
            P("mdl", None),
            P("rep", None, "mdl"),
            P("rep", "mdl", None),
            P("mdl", None),
            P("mdl", None),
        ),
        check_vma=False,
    )
```

```python
import functools

import jax
import jax.numpy as jnp
from jax import lax
from jax.experimental import pallas as pl
from jax.experimental.pallas import tpu as pltpu
from jax.sharding import PartitionSpec as P

HIGH = lax.Precision.HIGH
HIGHEST = lax.Precision.HIGHEST
MESH = pl.DeviceIdType.MESH
VMEM_LIMIT = 48 * 1024 * 1024


def position(chips, depth):
    me = lax.axis_index("rep")
    core = lax.rem(me, 2)
    chip = me // 2
    z = lax.axis_index("mdl")
    return me, core, chip, z


def remote(src, dst, send, recv, rep, z):
    return pltpu.make_async_remote_copy(
        src_ref=src,
        dst_ref=dst,
        send_sem=send,
        recv_sem=recv,
        device_id=(rep, z),
        device_id_type=MESH,
    )


def greet(chips, depth):
    me, core, chip, z = position(chips, depth)
    barrier = pltpu.get_barrier_semaphore()
    peers = [(chip * 2 + 1 - core, z)]
    for k in range(1, chips):
        peers.append((lax.rem(chip + k, chips) * 2 + core, z))
    for j in range(1, depth):
        peers.append((me, lax.rem(z + j, depth)))
    for peer in peers:
        pl.semaphore_signal(barrier, inc=1, device_id=peer, device_id_type=MESH)
    pl.semaphore_wait(barrier, len(peers))


def table_kernel(chips, depth, rows_ref, gain_ref, dy_ref, out_ref, gout_ref, dout_ref, sz, rz, sg, rg, sp, rp, sc, rc, sd, rd, local):
    me, core, chip, z = position(chips, depth)
    sibling = chip * 2 + 1 - core
    width = rows_ref.shape[2]

    def spot(owner, src):
        return out_ref.at[owner, :, pl.ds(pl.multiple_of(src * width, 128), width)]

    own = pltpu.make_async_copy(
        rows_ref, out_ref.at[:, :, pl.ds(pl.multiple_of(z * width, 128), width)], local.at[0]
    )
    own.start()
    own_gain = pltpu.make_async_copy(gain_ref, gout_ref.at[z], local.at[1])
    own_gain.start()
    own_dy = pltpu.make_async_copy(
        dy_ref, dout_ref.at[:, pl.ds(pl.multiple_of(z * width, 128), width)], local.at[2]
    )
    own_dy.start()
    greet(chips, depth)
    sends = []
    along = {}
    for j in range(1, depth):
        to = lax.rem(z + j, depth)
        copy = remote(rows_ref.at[me], spot(me, z), sz.at[j], rz.at[j], me, to)
        copy.start()
        gain = remote(gain_ref, gout_ref.at[z], sg.at[j], rg.at[j], me, to)
        gain.start()
        along[j] = (copy, gain)
        sends += [copy, gain]
    waits = []
    for j in range(1, depth):
        copy = remote(
            dy_ref,
            dout_ref.at[:, pl.ds(pl.multiple_of(z * width, 128), width)],
            sd.at[j],
            rd.at[j],
            me,
            lax.rem(z + j, depth),
        )
        copy.start()
        waits.append(copy)
        sends.append(copy)
    plane = {}
    for j in range(1, depth):
        along[j][0].wait_recv()
        src = lax.rem(z - j + depth, depth)
        piece = spot(me, src)
        for k in range(1, chips):
            to = lax.rem(chip + k, chips) * 2 + core
            copy = remote(piece, piece, sp.at[k, j], rp.at[k, j], to, z)
            copy.start()
            plane[k, j] = copy
            sends.append(copy)
        copy = remote(piece, piece, sc.at[0, j], rc.at[0, j], sibling, z)
        copy.start()
        waits.append(copy)
        sends.append(copy)
    for j in range(1, depth):
        src = lax.rem(z - j + depth, depth)
        for k in range(1, chips):
            plane[k, j].wait_recv()
            owner = lax.rem(chip - k + chips, chips) * 2 + core
            piece = spot(owner, src)
            copy = remote(piece, piece, sc.at[k, j], rc.at[k, j], sibling, z)
            copy.start()
            waits.append(copy)
            sends.append(copy)
    own.wait()
    own_gain.wait()
    own_dy.wait()
    for j in range(1, depth):
        along[j][1].wait_recv()
    for copy in waits:
        copy.wait_recv()
    for copy in sends:
        copy.wait_send()


def gather_table(embedding, norm_gain, dy_part, replicas, depth):
    chips = replicas // 2
    vocab, width = embedding.shape
    rows = embedding.reshape(replicas, vocab // replicas, width)
    gain = jnp.broadcast_to(norm_gain[None, :], (16, width))
    whole = jax.ShapeDtypeStruct(rows.shape[:2] + (depth * width,), rows.dtype)
    gains = jax.ShapeDtypeStruct((depth, 16, width), gain.dtype)
    sem = pltpu.SemaphoreType.DMA
    dy_all = jax.ShapeDtypeStruct((dy_part.shape[0], depth * width), dy_part.dtype)
    table, gains, dy_part = pl.pallas_call(
        functools.partial(table_kernel, chips, depth),
        out_shape=(whole, gains, dy_all),
        in_specs=[pl.BlockSpec(memory_space=pltpu.VMEM)] * 3,
        out_specs=[pl.BlockSpec(memory_space=pltpu.VMEM)] * 3,
        scratch_shapes=[
            sem((depth,)),
            sem((depth,)),
            sem((depth,)),
            sem((depth,)),
            sem((chips, depth)),
            sem((chips, depth)),
            sem((chips, depth)),
            sem((chips, depth)),
            sem((depth,)),
            sem((depth,)),
            sem((3,)),
        ],
        compiler_params=pltpu.CompilerParams(
            collective_id=0, has_side_effects=True, vmem_limit_bytes=VMEM_LIMIT
        ),
    )(rows, gain, dy_part)
    table = table.reshape(vocab, depth * width)
    return table, gains[:, 0, :].reshape(depth * width), dy_part


def reduce_steps(chips, depth, p_ref, out_ref, b1, b2, b3, sems, between):
    s1, r1, s2, r2, s3, r3, s4, r4, s5, r5, s6, r6 = sems
    me, core, chip, z = position(chips, depth)
    sibling = chip * 2 + 1 - core
    greet(chips, depth)
    sends = []
    first = remote(p_ref.at[1 - core], b1, s1.at[0], r1.at[0], sibling, z)
    first.start()
    sends.append(first)
    between(0)
    first.wait_recv()
    kind = p_ref.dtype
    b1[...] = (b1[...].astype(jnp.float32) + p_ref[core].astype(jnp.float32)).astype(kind)
    group = []
    for k in range(1, chips):
        to = lax.rem(chip + k, chips)
        copy = remote(b1.at[to], b2.at[chip], s2.at[k], r2.at[k], to * 2 + core, z)
        copy.start()
        group.append(copy)
    sends += group
    between(1)
    total = b1[chip].astype(jnp.float32)
    for k in range(1, chips):
        group[k - 1].wait_recv()
        total = total + b2[lax.rem(chip - k + chips, chips)].astype(jnp.float32)
    if depth > 1:
        b2[chip] = total.astype(kind)
        group = []
        for j in range(1, depth):
            to = lax.rem(z + j, depth)
            copy = remote(b2.at[chip, to], b3.at[z], s3.at[j], r3.at[j], me, to)
            copy.start()
            group.append(copy)
        sends += group
        total = b2[chip, z].astype(jnp.float32)
        for j in range(1, depth):
            group[j - 1].wait_recv()
            total = total + b3[lax.rem(z - j + depth, depth)].astype(jnp.float32)
        out_ref[core, chip, z] = total.astype(kind)
    else:
        out_ref[core, chip] = total.astype(kind)
    zz = z if depth > 1 else 0
    along = {}
    for j in range(1, depth):
        piece = out_ref.at[core, chip, zz]
        copy = remote(piece, piece, s4.at[j], r4.at[j], me, lax.rem(z + j, depth))
        copy.start()
        along[j] = copy
        sends.append(copy)
    waits = []
    plane = {}
    for j in range(depth):
        if j:
            along[j].wait_recv()
        src = lax.rem(zz - j + depth, depth) if depth > 1 else 0
        piece = out_ref.at[core, chip, src]
        for k in range(1, chips):
            to = lax.rem(chip + k, chips) * 2 + core
            copy = remote(piece, piece, s5.at[k, j], r5.at[k, j], to, z)
            copy.start()
            plane[k, j] = copy
            sends.append(copy)
        copy = remote(piece, piece, s6.at[0, j], r6.at[0, j], sibling, z)
        copy.start()
        waits.append(copy)
        sends.append(copy)
    between(2)
    for j in range(depth):
        src = lax.rem(zz - j + depth, depth) if depth > 1 else 0
        for k in range(1, chips):
            plane[k, j].wait_recv()
            piece = out_ref.at[core, lax.rem(chip - k + chips, chips), src]
            copy = remote(piece, piece, s6.at[k, j], r6.at[k, j], sibling, z)
            copy.start()
            waits.append(copy)
            sends.append(copy)
    between(3)
    for copy in waits:
        copy.wait_recv()
    for copy in sends:
        copy.wait_send()


def reduce_scratch(chips, depth, rows, kind):
    sem = pltpu.SemaphoreType.DMA
    return [
        pltpu.VMEM((chips, depth, rows, 128), kind),
        pltpu.VMEM((chips, depth, rows, 128), kind),
        pltpu.VMEM((depth, rows, 128), kind),
        sem((1,)),
        sem((1,)),
        sem((chips,)),
        sem((chips,)),
        sem((depth,)),
        sem((depth,)),
        sem((depth,)),
        sem((depth,)),
        sem((chips, depth)),
        sem((chips, depth)),
        sem((chips, depth)),
        sem((chips, depth)),
    ]


def left_kernel(chips, depth, p_ref, out_ref, b1, b2, b3, *sems):
    reduce_steps(chips, depth, p_ref, out_ref, b1, b2, b3, sems, lambda stage: None)


def reduce_left(p, replicas, depth):
    chips = replicas // 2
    rows = p.shape[0] // (2 * chips * depth)
    shape = (2, chips, depth, rows, 128)
    out = pl.pallas_call(
        functools.partial(left_kernel, chips, depth),
        out_shape=jax.ShapeDtypeStruct(shape, p.dtype),
        in_specs=[pl.BlockSpec(memory_space=pltpu.VMEM)],
        out_specs=pl.BlockSpec(memory_space=pltpu.VMEM),
        scratch_shapes=reduce_scratch(chips, depth, rows, p.dtype),
        compiler_params=pltpu.CompilerParams(
            collective_id=1, has_side_effects=True, vmem_limit_bytes=VMEM_LIMIT
        ),
    )(p.reshape(shape))
    return out.reshape(p.shape)


def factor_steps(work, rank, begin, end):
    tiles = [[work[h * rank + 8 * t : h * rank + 8 * t + 8, :] for t in range(rank // 8)] for h in range(2)]
    lines = lax.broadcasted_iota(jnp.int32, (8, 128), 0)
    for j in range(begin, end):
        at, line = divmod(j, 8)
        for h in range(2):
            lane = j + (rank if h == 0 else 0)
            part = tiles[h]
            row = part[at][line : line + 1, :]
            columns = [
                jnp.broadcast_to(part[t][:, lane : lane + 1], (8, 128))
                for t in range(at, rank // 8)
            ]
            scaled = row * (1.0 / columns[0][line : line + 1, :])
            for t in range(at, rank // 8):
                fresh = part[t] - columns[t - at] * scaled
                if t == at:
                    fresh = jnp.where(lines > line, fresh, part[t])
                part[t] = fresh
    for h in range(2):
        for t in range(rank // 8):
            work[h * rank + 8 * t : h * rank + 8 * t + 8, :] = tiles[h][t]


def right_kernel(chips, rank, p_ref, gram_ref, out_ref, low_ref, b1, b2, b3, work, *sems):
    def between(stage):
        if stage == 0:
            work[...] = gram_ref[...]
        factor_steps(work, rank, stage * rank // 4, (stage + 1) * rank // 4)

    reduce_steps(chips, 1, p_ref, out_ref, b1, b2, b3, sems, between)
    lanes = lax.broadcasted_iota(jnp.int32, (rank, 128), 1)
    lines = lax.broadcasted_iota(jnp.int32, (rank, 128), 0)
    top = work[:rank, :]
    pivots = jnp.sum(jnp.where(lanes == lines + rank, top, 0.0), axis=1, keepdims=True)
    low_ref[:rank, :] = jnp.where(lanes < rank, top / jnp.sqrt(pivots), 0.0)
    end = work[rank:, :]
    pivots = jnp.sum(jnp.where(lanes == lines, end, 0.0), axis=1, keepdims=True)
    low_ref[rank:, :] = jnp.where(lanes >= rank, end / jnp.sqrt(pivots), 0.0)


def reduce_right(p, gram, replicas):
    chips = replicas // 2
    rank = gram.shape[0] // 2
    rows = p.shape[0] // (2 * chips)
    shape = (2, chips, 1, rows, 128)
    eye = jnp.eye(rank, dtype=jnp.float32)
    start = jnp.concatenate(
        [
            jnp.concatenate([eye, gram[:rank, :rank]], axis=1),
            jnp.concatenate([gram[rank:, rank:], eye], axis=1),
        ],
        axis=0,
    )
    out, low = pl.pallas_call(
        functools.partial(right_kernel, chips, rank),
        out_shape=(
            jax.ShapeDtypeStruct(shape, jnp.float32),
            jax.ShapeDtypeStruct((2 * rank, 128), jnp.float32),
        ),
        in_specs=[pl.BlockSpec(memory_space=pltpu.VMEM)] * 2,
        out_specs=[pl.BlockSpec(memory_space=pltpu.VMEM)] * 2,
        scratch_shapes=(lambda s: s[:3] + [pltpu.VMEM((2 * rank, 128), jnp.float32)] + s[3:])(
            reduce_scratch(chips, 1, rows, p.dtype)
        ),
        compiler_params=pltpu.CompilerParams(
            collective_id=2, has_side_effects=True, vmem_limit_bytes=VMEM_LIMIT
        ),
    )(p.reshape(shape), start)
    return out.reshape(p.shape), low


def shards(
    replicas,
    depth,
    token_ids,
    lengths,
    embedding,
    norm_gain,
    scores,
    cotangent,
    w_value,
    w_out,
    err_value,
    err_out,
    q_value,
    q_out,
):
    samples, seq = token_ids.shape
    vocab = embedding.shape[0]
    rows = samples * seq
    rank = q_value.shape[1]
    flat_dy = cotangent.reshape(rows, -1)
    held = rows - rows // 4
    dy_most = lax.all_gather(flat_dy[:held], "mdl", axis=1, tiled=True)
    width_full = dy_most.shape[1]
    raw, gain, dy_rest = gather_table(embedding, norm_gain, flat_dy[held:], replicas, depth)
    raw = raw.astype(jnp.float32)
    scale = lax.rsqrt(jnp.sum(raw * raw, axis=1) / width_full + 1e-06)
    table = (raw * scale[:, None] * gain.astype(jnp.float32)[None, :]).astype(jnp.bfloat16)
    flat_ids = token_ids.reshape(rows)
    onehot = (flat_ids[:, None] == jnp.arange(vocab, dtype=jnp.int32)[None, :]).astype(jnp.bfloat16)
    normed = jnp.dot(onehot, table, preferred_element_type=jnp.float32).astype(jnp.bfloat16)
    live = jnp.arange(seq, dtype=jnp.int32)[None, :] < lengths[:, None]
    heads_local = scores.shape[1]
    inner_local = w_value.shape[1]
    head_size = inner_local // heads_local
    values = jnp.dot(normed, w_value, preferred_element_type=jnp.float32).astype(jnp.bfloat16)
    logits = jnp.where(live[:, None, None, :], scores.astype(jnp.float32), jnp.float32(-1e30))
    top = jnp.max(logits, axis=-1, keepdims=True)
    expo = jnp.exp(logits - top)
    weights = (expo / jnp.sum(expo, axis=-1, keepdims=True)).astype(jnp.bfloat16)
    values4 = values.reshape(samples, seq, heads_local, head_size)
    context = (
        jnp.einsum("shqk,skhd->sqhd", weights, values4, preferred_element_type=jnp.float32)
        .astype(jnp.bfloat16)
        .reshape(rows, inner_local)
    )
    dy_whole = jnp.concatenate([dy_most, dy_rest], axis=0)
    dy_rows = jnp.where(live.reshape(rows, 1), dy_whole, jnp.zeros_like(dy_whole))
    dcontext = lax.dot_general(
        dy_rows, w_out, (((1,), (1,)), ((), ())), preferred_element_type=jnp.float32
    ).astype(jnp.bfloat16)
    dctx4 = dcontext.reshape(samples, seq, heads_local, head_size)
    dvalues = (
        jnp.einsum("shqk,sqhd->skhd", weights, dctx4, preferred_element_type=jnp.float32)
        .astype(jnp.bfloat16)
        .reshape(rows, inner_local)
    )
    grad_out = lax.dot_general(
        context, dy_rows, (((0,), (0,)), ((), ())), preferred_element_type=jnp.float32
    )
    grad_value = lax.dot_general(
        normed, dvalues, (((0,), (0,)), ((), ())), preferred_element_type=jnp.float32
    )
    mem_value = grad_value + err_value[0].astype(jnp.float32)
    mem_out = grad_out + err_out[0].astype(jnp.float32)
    kept_value = mem_value.astype(jnp.bfloat16)
    kept_out = mem_out.astype(jnp.bfloat16)
    none = jnp.zeros_like(q_value)
    right_value = jnp.concatenate([q_value, none], axis=1).astype(jnp.bfloat16)
    right_out = jnp.concatenate([none, q_out], axis=1).astype(jnp.bfloat16)
    part = jnp.dot(kept_value, right_value, preferred_element_type=jnp.float32)
    part = part + lax.dot_general(
        kept_out, right_out, (((0,), (0,)), ((), ())), preferred_element_type=jnp.float32
    )
    p_both = reduce_left(part.astype(jnp.bfloat16), replicas, depth)
    gram = lax.dot_general(
        p_both, p_both, (((0,), (0,)), ((), ())), preferred_element_type=jnp.float32
    )
    first = jnp.arange(2 * rank)[None, :] < rank
    nothing = jnp.zeros_like(p_both)
    term = lax.dot_general(
        kept_value,
        jnp.where(first, p_both, nothing),
        (((0,), (0,)), ((), ())),
        preferred_element_type=jnp.float32,
    )
    term = term + jnp.dot(
        kept_out, jnp.where(first, nothing, p_both), preferred_element_type=jnp.float32
    )
    terms, low = reduce_right(term, gram, replicas)
    phat = lax.dot_general(
        p_both.astype(jnp.float32), low, (((1,), (1,)), ((), ())), precision=HIGH
    )
    new_q = lax.dot_general(terms, low, (((1,), (1,)), ((), ())), precision=HIGHEST) / replicas
    new_q_value = new_q[:, :rank]
    new_q_out = new_q[:, rank:]
    rough_phat = phat.astype(jnp.bfloat16)
    rough_q = new_q.astype(jnp.bfloat16)
    full_value = lax.dot_general(
        rough_phat[:, :rank],
        rough_q[:, :rank],
        (((1,), (1,)), ((), ())),
        preferred_element_type=jnp.float32,
    )
    full_out = lax.dot_general(
        rough_q[:, rank:],
        rough_phat[:, rank:],
        (((1,), (1,)), ((), ())),
        preferred_element_type=jnp.float32,
    )
    new_err_value = (mem_value - full_value).astype(jnp.bfloat16)[None]
    new_err_out = (mem_out - full_out).astype(jnp.bfloat16)[None]
    return (
        full_value.astype(jnp.bfloat16),
        full_out.astype(jnp.bfloat16),
        new_err_value,
        new_err_out,
        new_q_value,
        new_q_out,
    )


def solution(mesh):
    return jax.shard_map(
        functools.partial(shards, mesh.shape["rep"], mesh.shape["mdl"]),
        mesh=mesh,
        in_specs=(
            P("rep", None),
            P("rep"),
            P(None, "mdl"),
            P("mdl"),
            P("rep", "mdl", None, None),
            P("rep", None, "mdl"),
            P(None, "mdl"),
            P("mdl", None),
            P("rep", None, "mdl"),
            P("rep", "mdl", None),
            P("mdl", None),
            P("mdl", None),
        ),
        out_specs=(
            P(None, "mdl"),
            P("mdl", None),
            P("rep", None, "mdl"),
            P("rep", "mdl", None),
            P("mdl", None),
            P("mdl", None),
        ),
        check_vma=False,
    )
```
